512 devices in a mesh: nodes: 64 (over z, y), rel: 8 (over x, core).
Axes of the slice: x: 4, y: 8, z: 8, core: 2. Of those that a mesh axis runs over, the one named last changes fastest.
Arguments:
- grad_out: bfloat16 [16384, 512], P('nodes'), may hold values from -6 to 6
- node_feats: bfloat16 [16384, 512], P('nodes'), may hold values from -6 to 6
- rel_weight: bfloat16 [16, 512, 512], P('rel'), may hold values from -0.25 to 0.25
- self_weight: bfloat16 [512, 512], replicated, may hold values from -0.25 to 0.25
- send_rows: int32 [16, 64, 64, 16], P('rel', 'nodes'), may hold values from 0 to 255
- recv_rows: int32 [16, 64, 64, 16], P('rel', 'nodes'), may hold values from 0 to 255
- send_counts: int32 [16, 64, 64], P('rel', 'nodes'), may hold values from 4 to 16, as said below
Outputs:
- grad_feats: bfloat16 [16384, 512], P(('nodes', 'rel'))
- grad_rel: bfloat16 [16, 512, 512], P('rel')
- grad_self: bfloat16 [512, 512], P('rel')
The draws below stay inside these ranges and needn't reach their ends.
Inputs may be any that keep to these rules, and one draw needn't show every extreme that they name: Only the first send_counts[r, b, p] slots of send_rows and recv_rows are edges. In every draw and relation some block p receives 16 live slots from every block.
All inputs are finite; a program needn't handle non-finite values.
Results may differ from the reference program's by a relative error of at most 0.0049.
Values may be sent and summed in bfloat16 or wider, within the bound.
A program may use at most 64 MiB of HBM per device.

```python
import jax
import jax.numpy as jnp
from jax import lax

D = 512
NODE_DEV = 256
CAP = 16
RELS = 16
NODES = 16384
N_NODES = 64


def draw_send_counts(key, part):
    key = jax.random.fold_in(key, 7)
    key_base, key_heavy, key_hub, key_full = jax.random.split(key, 4)
    shape = (RELS, N_NODES, N_NODES)
    base_count = jax.random.randint(key_base, shape, CAP // 4, CAP // 2 + 1)
    heavy_count = jax.random.randint(key_heavy, shape, 3 * CAP // 4, CAP + 1)
    hub_flag = jax.random.randint(key_hub, (RELS, N_NODES, 1), 0, 8) == 0
    counts = jnp.where(hub_flag, heavy_count, base_count)
    full_peer = jax.random.randint(key_full, (RELS, 1, 1), 0, N_NODES)
    peer_index = lax.broadcasted_iota(jnp.int32, shape, 2)
    counts = jnp.where(peer_index == full_peer, CAP, counts)
    return counts.astype(jnp.int32)


def place_ends(result, rng, least, largest):
    longest = result.shape.index(max(result.shape))
    spots = []
    for shift in (0, 1):
        where = [jax.random.randint(jax.random.fold_in(rng, axis), (), 0, length) for axis, length in enumerate(result.shape)]
        where[longest] = (where[longest] + shift) % result.shape[longest]
        spots.append(tuple(where))
    return result.at[spots[0]].set(least).at[spots[1]].set(largest)


def shard_levels(own_key, extent, shards, low, high):
    gain, own = 1.0, jax.random.fold_in(own_key, 6)
    for axis_at, blocks in shards:
        draws = jnp.exp(jax.random.uniform(jax.random.fold_in(own, axis_at), (blocks,), jnp.float32, low / len(shards), high / len(shards)))
        gain = gain * jnp.repeat(draws, extent[axis_at] // blocks).reshape([-1 if axis == axis_at else 1 for axis in range(len(extent))])
    return gain


def bell_draw(key, extent, spread, most, cuts=(), held_as=jnp.bfloat16):
    array = jax.random.normal(key, extent, jnp.float32) * spread
    if len(cuts) > 0:
        array = shard_levels(key, extent, cuts, -0.22, 0.18) * array
    return jnp.clip(array, min=-most, max=most).astype(held_as)


def setup_inputs(seed: int = 0) -> dict:
    key_list = jax.random.split(jax.random.key(seed), 8)
    return {
        "grad_out": bell_draw(key_list[0], (NODES, D), 1.0, 6.0, ((0, 64),)),
        "node_feats": bell_draw(key_list[1], (NODES, D), 1.0, 6.0, ((0, 64),)),
        "rel_weight": bell_draw(key_list[2], (RELS, D, D), D ** -0.5, 0.25, ((0, 8),)),
        "self_weight": bell_draw(key_list[3], (D, D), D ** -0.5, 0.25),
        "send_rows": place_ends(jax.random.randint(key_list[4], (RELS, N_NODES, N_NODES, CAP), 0, NODE_DEV), jax.random.fold_in(key_list[4], 1), 0, NODE_DEV - 1).astype(jnp.int32),
        "recv_rows": place_ends(jax.random.randint(key_list[5], (RELS, N_NODES, N_NODES, CAP), 0, NODE_DEV), jax.random.fold_in(key_list[5], 1), 0, NODE_DEV - 1).astype(jnp.int32),
        "send_counts": draw_send_counts(jax.random.fold_in(key_list[7], 71), 0),
    }


def reference(grad_out, node_feats, rel_weight, self_weight, send_rows, recv_rows, send_counts):
    def one_relation(total, items):
        rows_r, targets_r, counts_r, weight_r = items
        live = (lax.broadcasted_iota(jnp.int32, rows_r.shape, 2) < counts_r[:, :, None]).reshape(-1)
        sender = lax.broadcasted_iota(jnp.int32, rows_r.shape, 0)
        receiver = lax.broadcasted_iota(jnp.int32, rows_r.shape, 1)
        dst_index = (sender * NODE_DEV + rows_r).reshape(-1).astype(jnp.int32)
        src_index = (receiver * NODE_DEV + targets_r).reshape(-1).astype(jnp.int32)
        degree = jax.ops.segment_sum(live.astype(jnp.float32), dst_index, num_segments=NODES)
        edge_norm = jnp.where(live, 1.0 / jnp.where(live, degree[dst_index], 1.0), 0.0)
        message = (edge_norm[:, None] * grad_out[dst_index].astype(jnp.float32)).astype(jnp.bfloat16)
        gathered = jax.ops.segment_sum(message.astype(jnp.float32), src_index, num_segments=NODES).astype(jnp.bfloat16)
        total = total + jnp.dot(gathered, weight_r.T, preferred_element_type=jnp.float32)
        weight_grad = jnp.dot(node_feats.T, gathered, preferred_element_type=jnp.float32)
        return total, weight_grad

    start = jnp.zeros((NODES, D), jnp.float32)
    total, rel_grads = lax.scan(one_relation, start, (send_rows, recv_rows, send_counts, rel_weight))
    scale = NODES ** -0.5
    self_term = jnp.dot(grad_out, self_weight.T, preferred_element_type=jnp.float32)
    grad_feats = (total + self_term).astype(jnp.bfloat16)
    grad_rel = (rel_grads * scale).astype(jnp.bfloat16)
    grad_self = (jnp.dot(node_feats.T, grad_out, preferred_element_type=jnp.float32) * scale).astype(jnp.bfloat16)
    return (grad_feats, grad_rel, grad_self)
```

```python
import functools

import jax
import jax.numpy as jnp
from jax import lax
from jax.experimental import pallas as pl
from jax.experimental.pallas import tpu as pltpu
from jax.sharding import PartitionSpec as P

MESH = pl.DeviceIdType.MESH
F32 = jnp.float32
BF16 = jnp.bfloat16

(MSG1A, MSG1B, TGT1, MSG2A, MSG2B, TGT2, RS1A, RS1B, RS2A, RS2B, AG1A, AG1B, AG2A, AG2B, FEAT) = range(15)
EXCHANGES = 15


def iota(shape, dim):
    return lax.broadcasted_iota(jnp.int32, shape, dim)


def dot(a, b, contract):
    return lax.dot_general(a, b, ((contract[0], contract[1]), ((), ())), preferred_element_type=F32)


def kernel(
    q, groups, scale,
    grad_ref, feat_ref, weight_ref, self_ref, rows_ref, targets_ref,
    out_feat, out_rel, out_self,
    send_a, send_b, mid_a, mid_b, last, tgt_mid, tgt_send, tgt_last, one_hot, feat_t, gathered, self_part, self_term,
    part, part_in, rs1_a, rs1_b, rs1_in_a, rs1_in_b, rs2_a, rs2_b, rs2_in_a, rs2_in_b, block_a, block_b, all_a, all_b,
    send_sem, recv_sem,
):
    rels, node_rows, width = gathered.shape
    slots = last.shape[3]
    half = width // 2
    lanes = q * slots
    n = lax.axis_index("nodes")
    k = lax.axis_index("rel")
    z, y = n // q, n % q
    low, high = slice(0, half), slice(half, width)

    def along(axis, j):
        return (j * q + y, k) if axis == "z" else ((z * q + j, k) if axis == "y" else (n, j))

    def place(axis):
        return (z, q) if axis == "z" else ((y, q) if axis == "y" else (k, groups))

    def copy(axis, row, step, source, target, peer):
        return pltpu.make_async_remote_copy(
            src_ref=source, dst_ref=target, send_sem=send_sem.at[row, step], recv_sem=recv_sem.at[row, step],
            device_id=along(axis, peer), device_id_type=MESH,
        )

    def start(axis, row, source, target):
        me, count = place(axis)

        def body(step, carry):
            peer = (me + step) % count
            copy(axis, row, step, source(peer), target, peer).start()
            return carry

        lax.fori_loop(1, count, body, 0)

    def finish(axis, row, source, landing):
        me, count = place(axis)

        def body(step, carry):
            peer = (me + count - step) % count
            copy(axis, row, step, source(peer), landing(peer), peer).wait()
            return carry

        lax.fori_loop(1, count, body, 0)

    barrier = pltpu.get_barrier_semaphore()
    for axis in ("z", "y", "rel"):
        me, count = place(axis)

        def greet(step, carry, axis=axis, me=me, count=count):
            pl.semaphore_signal(barrier, inc=1, device_id=along(axis, (me + step) % count), device_id_type=MESH)
            return carry

        lax.fori_loop(1, count, greet, 0)

    node = iota((node_rows, lanes), 0)
    grad = grad_ref[...]
    for r in range(rels):
        hits = jnp.zeros((node_rows, lanes), F32)
        for b in range(q):
            hits = hits + (rows_ref[r, b : b + 1, :] == node).astype(F32)
        degree = jnp.sum(hits, axis=1, keepdims=True)
        inverse = 1.0 / jnp.maximum(degree, 1.0)
        message = (grad.astype(F32) * inverse).astype(BF16)
        for b in range(q):
            pick = (rows_ref[r, b : b + 1, :] == node).astype(BF16)
            picked = dot(pick, message, ((0,), (0,))).astype(BF16)
            send_a[b, :, r] = picked[:, low].reshape(q, slots, half)
            send_b[:, b, r] = picked[:, high].reshape(q, slots, half)

    pl.semaphore_wait(barrier, 2 * (q - 1) + groups - 1)
    start("z", TGT1, lambda j: targets_ref.at[j], tgt_mid.at[z])
    start("z", MSG1A, lambda j: send_a.at[j], mid_a.at[z])
    start("y", MSG1B, lambda j: send_b.at[j], mid_b.at[y])

    mid_a[z] = send_a[z]
    mid_b[y] = send_b[y]
    tgt_mid[z] = targets_ref[z]
    feat_t[...] = feat_ref[...].T
    self_part[...] = dot(feat_t[...], grad, ((1,), (0,)))
    own_rows = node_rows // groups
    own = pl.ds(pl.multiple_of(k * own_rows, own_rows), own_rows)
    self_term[...] = dot(grad_ref[own, :], self_ref[...], ((1,), (1,)))

    finish("z", TGT1, lambda j: targets_ref.at[j], lambda j: tgt_mid.at[j])
    spread = q * lanes
    same_slot = iota((lanes, spread), 0) == (iota((lanes, spread), 1) // lanes) * slots + iota((lanes, spread), 1) % slots
    same_from = iota((q, spread), 0) == (iota((q, spread), 1) // slots) % q
    for r in range(rels):
        copies = dot(tgt_mid[:, r, :].astype(BF16), same_slot.astype(BF16), ((1,), (0,)))
        row = jnp.sum(jnp.where(same_from, copies, 0.0), axis=0, keepdims=True)
        for b in range(q):
            tgt_send[b, r : r + 1, :] = row[:, b * lanes : (b + 1) * lanes]
    start("y", TGT2, lambda j: tgt_send.at[j], tgt_last.at[y])
    tgt_last[y] = tgt_send[y]

    finish("z", MSG1A, lambda j: send_a.at[j], lambda j: mid_a.at[j])
    start("y", MSG2A, lambda j: mid_a.at[:, j], last.at[y, :, :, :, low])
    finish("y", MSG1B, lambda j: send_b.at[j], lambda j: mid_b.at[j])
    start("z", MSG2B, lambda j: mid_b.at[:, j], last.at[:, z, :, :, high])
    last[y, :, :, :, low] = mid_a[:, y]
    last[:, z, :, :, high] = mid_b[:, z]

    finish("y", TGT2, lambda j: tgt_send.at[j], lambda j: tgt_last.at[j])
    for r in range(rels):
        for b in range(q):
            one_hot[r, :, b * lanes : (b + 1) * lanes] = (
                tgt_last[b, r : r + 1, :].astype(jnp.int32) == node
            ).astype(BF16)

    finish("y", MSG2A, lambda j: mid_a.at[:, j], lambda j: last.at[j, :, :, :, low])
    finish("z", MSG2B, lambda j: mid_b.at[:, j], lambda j: last.at[:, j, :, :, high])

    rel_rows = rels * width // q
    sub_rows = rel_rows // q
    self_rows = width // groups
    strip = self_rows // q
    own_self = self_part[pl.ds(pl.multiple_of(k * self_rows, self_rows), self_rows), :]
    pad = jnp.zeros((16 - strip, width), F32)
    for b in range(q):
        tail = jnp.concatenate([own_self[b * strip : (b + 1) * strip], pad], axis=0).astype(BF16)
        rs1_a[b, rel_rows:, :] = tail[:, low]
        rs1_b[b, rel_rows:, :] = tail[:, high]
    for r in range(rels):
        arrived = last[:, :, r].reshape(q * lanes, width)
        gathered[r] = dot(one_hot[r], arrived, ((1,), (0,))).astype(BF16)
        grads = dot(feat_t[...], gathered[r], ((1,), (0,))).astype(BF16)
        for b in range(width // rel_rows):
            at = r * (width // rel_rows) + b
            rs1_a[at, :rel_rows, :] = grads[b * rel_rows : (b + 1) * rel_rows, low]
            rs1_b[at, :rel_rows, :] = grads[b * rel_rows : (b + 1) * rel_rows, high]
    start("y", RS1A, lambda j: rs1_a.at[j], rs1_in_a.at[y])
    start("z", RS1B, lambda j: rs1_b.at[j], rs1_in_b.at[z])
    rs1_in_a[y] = rs1_a[y]
    rs1_in_b[z] = rs1_b[z]

    total = dot(gathered[0], weight_ref[0], ((1,), (1,)))
    for r in range(1, rels):
        total = total + dot(gathered[r], weight_ref[r], ((1,), (1,)))
    part[...] = total.reshape(groups, own_rows, width)
    start("rel", FEAT, lambda j: part.at[j], part_in.at[k])
    part_in[k] = part[k]

    def second(blocks, sends):
        total = blocks[0].astype(F32)
        for b in range(1, q):
            total = total + blocks[b].astype(F32)
        for b in range(q):
            sends[b] = jnp.concatenate(
                [total[b * sub_rows : (b + 1) * sub_rows], total[rel_rows:]], axis=0
            ).astype(BF16)

    def third(blocks, block, me):
        total = blocks[0].astype(F32)
        for b in range(1, q):
            total = total + blocks[b].astype(F32)
        total = (total * scale).astype(BF16)
        block[pl.ds(pl.multiple_of(me * sub_rows, sub_rows), sub_rows), :] = total[:sub_rows]
        block[rel_rows:, :] = total[sub_rows:]

    def piece(block):
        return lambda j: block.at[pl.ds(pl.multiple_of(j * sub_rows, sub_rows), sub_rows), :]

    finish("y", RS1A, lambda j: rs1_a.at[j], lambda j: rs1_in_a.at[j])
    second(rs1_in_a, rs2_a)
    start("z", RS2A, lambda j: rs2_a.at[j], rs2_in_a.at[z])
    finish("z", RS1B, lambda j: rs1_b.at[j], lambda j: rs1_in_b.at[j])
    second(rs1_in_b, rs2_b)
    start("y", RS2B, lambda j: rs2_b.at[j], rs2_in_b.at[y])
    rs2_in_a[z] = rs2_a[z]
    rs2_in_b[y] = rs2_b[y]

    finish("z", RS2A, lambda j: rs2_a.at[j], lambda j: rs2_in_a.at[j])
    third(rs2_in_a, block_a, z)
    start("z", AG1A, lambda j: piece(block_a)(z), piece(block_a)(z))
    finish("y", RS2B, lambda j: rs2_b.at[j], lambda j: rs2_in_b.at[j])
    third(rs2_in_b, block_b, y)
    start("y", AG1B, lambda j: piece(block_b)(y), piece(block_b)(y))

    finish("z", AG1A, lambda j: piece(block_a)(z), piece(block_a))
    start("y", AG2A, lambda j: block_a, all_a.at[y])
    finish("y", AG1B, lambda j: piece(block_b)(y), piece(block_b))
    start("z", AG2B, lambda j: block_b, all_b.at[z])
    all_a[y] = block_a[...]
    all_b[z] = block_b[...]

    finish("rel", FEAT, lambda j: part.at[j], lambda j: part_in.at[j])
    total = self_term[...]
    for b in range(groups):
        total = total + part_in[b]
    out_feat[...] = total.astype(BF16)

    finish("y", AG2A, lambda j: block_a, lambda j: all_a.at[j])
    finish("z", AG2B, lambda j: block_b, lambda j: all_b.at[j])
    for blocks, side in ((all_a, low), (all_b, high)):
        for b in range(q):
            out_rel[b * rel_rows : (b + 1) * rel_rows, side] = blocks[b, :rel_rows, :]
        strips = [blocks[b, rel_rows:, :].astype(F32)[:strip] for b in range(q)]
        out_self[:, side] = jnp.concatenate(strips, axis=0).astype(BF16)


def solution(mesh):
    q = int(round(mesh.shape["nodes"] ** 0.5))
    groups = mesh.shape["rel"]

    def per_device(grad_out, node_feats, rel_weight, self_weight, send_rows, recv_rows, send_counts):
        node_rows, width = grad_out.shape
        rels = rel_weight.shape[0]
        slots = send_rows.shape[3]
        half, lanes = width // 2, q * slots
        rel_rows = rels * width // q
        sub_rows = rel_rows // q
        live = iota((rels, q * q, slots), 2) < send_counts.reshape(rels, q * q, 1)
        rows = jnp.where(live, send_rows.reshape(rels, q * q, slots), -1).reshape(rels, q, lanes)
        targets = jnp.where(live, recv_rows.reshape(rels, q * q, slots), -1).reshape(rels, q, lanes)
        targets = jnp.pad(targets.astype(F32).transpose(1, 0, 2), ((0, 0), (0, 8 - rels), (0, 0)))
        in_vmem = pl.BlockSpec(memory_space=pltpu.VMEM)
        pair = (q, q, rels, slots, half)
        flops = 2 * width * (3 * rels * node_rows * q * lanes + 3 * rels * node_rows * width)
        outs = pl.pallas_call(
            functools.partial(kernel, q, groups, (node_rows * q * q) ** (-0.5)),
            out_shape=(
                jax.ShapeDtypeStruct((node_rows // groups, width), BF16),
                jax.ShapeDtypeStruct((rels * width, width), BF16),
                jax.ShapeDtypeStruct((width // groups, width), BF16),
            ),
            in_specs=[in_vmem] * 6,
            out_specs=(in_vmem,) * 3,
            scratch_shapes=[
                pltpu.VMEM(pair, BF16), pltpu.VMEM(pair, BF16),
                pltpu.VMEM(pair, BF16), pltpu.VMEM(pair, BF16),
                pltpu.VMEM((q, q, rels, slots, width), BF16),
                pltpu.VMEM((q, 8, lanes), F32), pltpu.VMEM((q, 8, lanes), F32), pltpu.VMEM((q, 8, lanes), F32),
                pltpu.VMEM((rels, node_rows, q * lanes), BF16),
                pltpu.VMEM((width, node_rows), BF16),
                pltpu.VMEM((rels, node_rows, width), BF16),
                pltpu.VMEM((width, width), F32),
                pltpu.VMEM((node_rows // groups, width), F32),
                pltpu.VMEM((groups, node_rows // groups, width), F32),
                pltpu.VMEM((groups, node_rows // groups, width), F32),
            ]
            + [pltpu.VMEM((q, rel_rows + 16, half), BF16)] * 4
            + [pltpu.VMEM((q, sub_rows + 16, half), BF16)] * 4
            + [pltpu.VMEM((rel_rows + 16, half), BF16)] * 2
            + [pltpu.VMEM((q, rel_rows + 16, half), BF16)] * 2
            + [
                pltpu.SemaphoreType.DMA((EXCHANGES, max(q, groups))),
                pltpu.SemaphoreType.DMA((EXCHANGES, max(q, groups))),
            ],
            compiler_params=pltpu.CompilerParams(
                collective_id=0, has_side_effects=True, vmem_limit_bytes=48 * 1024 * 1024
            ),
            cost_estimate=pl.CostEstimate(flops=flops, bytes_accessed=4 * 1024 * 1024, transcendentals=0),
        )(grad_out, node_feats, rel_weight, self_weight, rows, targets)
        return outs[0], outs[1].reshape(rels, width, width), outs[2]

    return jax.shard_map(
        per_device,
        mesh=mesh,
        in_specs=(
            P("nodes", None),
            P("nodes", None),
            P("rel", None, None),
            P(),
            P("rel", "nodes", None, None),
            P("rel", "nodes", None, None),
            P("rel", "nodes", None),
        ),
        out_specs=(P(("nodes", "rel"), None), P("rel", None, None), P("rel", None)),
        check_vma=False,
    )
```

```python
import functools

import jax
import jax.numpy as jnp
from jax import lax
from jax.experimental import pallas as pl
from jax.experimental.pallas import tpu as pltpu
from jax.sharding import PartitionSpec as P

MESH = pl.DeviceIdType.MESH
F32 = jnp.float32
BF16 = jnp.bfloat16

META, RAW, CORE, PART, SUM1, SUM2, ALL1, ALL2, TGT, SELF1, SELF2, SELF3, FEAT = 0, 2, 4, 6, 14, 18, 22, 26, 30, 31, 32, 33, 34
EXCHANGES = 35


def iota(shape, dim):
    return lax.broadcasted_iota(jnp.int32, shape, dim)


def dot(a, b, contract):
    return lax.dot_general(a, b, ((contract[0], contract[1]), ((), ())), preferred_element_type=F32)


def kernel(
    q, groups, scale,
    grad_hbm, feat_hbm, weight_hbm, self_hbm, rows_hbm, targets_hbm, counts_hbm,
    out_feat, out_rel, out_self,
    grad, feat, weight, self_w, rows, targets, counts,
    meta_a, meta_b, meta_in_a, meta_in_b, raw_a, raw_b, part_a, part_b, last,
    tgt_send, tgt_last, one_hot, feat_t, gathered, self_all, self1, self1_in, self2, self2_in, self3, self3_in,
    self_term, share, share_in, sum1_a, sum1_b, sum1_in_a, sum1_in_b, sum2_a, sum2_b, sum2_in_a, sum2_in_b,
    block_a, block_b, all_a, all_b,
    send_sem, recv_sem, load_sem,
):
    rels, node_rows, width = gathered.shape
    slots = last.shape[3]
    half, lanes, cut = width // 2, q * slots, q // 2
    n = lax.axis_index("nodes")
    k = lax.axis_index("rel")
    z, y, core = n // q, n % q, k % 2
    low, high = slice(0, half), slice(half, width)

    loads = [
        pltpu.make_async_copy(source, target, load_sem.at[i])
        for i, (source, target) in enumerate((
            (rows_hbm, rows), (counts_hbm, counts), (targets_hbm, targets), (grad_hbm, grad),
            (feat_hbm, feat), (self_hbm, self_w), (weight_hbm, weight),
        ))
    ]
    for load in loads:
        load.start()

    def offset(t, count):
        near = (t + 1) // 2
        return (t % 2) * near + (1 - t % 2) * (count - near)

    def along(axis, j):
        return (j * q + y, k) if axis == "z" else ((z * q + j, k) if axis == "y" else (n, j))

    def place(axis):
        return (z, q) if axis == "z" else ((y, q) if axis == "y" else (k, groups))

    def copy(row, t, source, target, device):
        return pltpu.make_async_remote_copy(
            src_ref=source, dst_ref=target, send_sem=send_sem.at[row, t], recv_sem=recv_sem.at[row, t],
            device_id=device, device_id_type=MESH,
        )

    def start(*items):
        def body(t, carry):
            for axis, row, source, target in items:
                me, count = place(axis)
                peer = (me + offset(t, count)) % count
                copy(row, t, source(peer), target(t), along(axis, peer)).start()
            return carry

        lax.fori_loop(1, place(items[0][0])[1], body, 0)

    def finish(*items):
        def body(t, carry):
            for axis, row, source, landing in items:
                me, count = place(axis)
                peer = (me + count - offset(t, count)) % count
                copy(row, t, source(peer), landing(t, peer), along(axis, peer)).wait()
            return carry

        lax.fori_loop(1, place(items[0][0])[1], body, 0)

    barrier = pltpu.get_barrier_semaphore()
    for axis in ("z", "y", "rel"):
        me, count = place(axis)

        def greet(t, carry, axis=axis, me=me, count=count):
            pl.semaphore_signal(barrier, inc=1, device_id=along(axis, (me + t) % count), device_id_type=MESH)
            return carry

        lax.fori_loop(1, count, greet, 0)

    node = iota((node_rows, lanes), 0)
    eye = iota((lanes, lanes), 0) == iota((lanes, lanes), 1)
    blocks = q * q
    spread = (iota((slots, lanes), 0) == iota((slots, lanes), 1) % slots).astype(BF16)
    from_z = iota((blocks, lanes), 0) // q == iota((blocks, lanes), 1) // slots
    from_y = iota((blocks, lanes), 0) % q == iota((blocks, lanes), 1) // slots
    block_eye = iota((blocks, blocks), 0) == iota((blocks, blocks), 1)
    meta_a[...] = jnp.zeros_like(meta_a)
    meta_b[...] = jnp.zeros_like(meta_b)
    for load in loads[:3]:
        load.wait()
    for r in range(rels):
        count = jnp.sum(jnp.where(block_eye, counts[r], 0), axis=1, keepdims=True)
        live = iota((blocks, slots), 1) < count
        picks = dot(jnp.where(live, rows[r], -1).astype(F32).astype(BF16), spread, ((1,), (0,)))
        adds = dot(jnp.where(live, targets[r], -1).astype(F32).astype(BF16), spread, ((1,), (0,)))
        pick_a = jnp.sum(jnp.where(from_y, picks, 0.0).reshape(q, q, lanes), axis=1)
        pick_b = jnp.sum(jnp.where(from_z, picks, 0.0).reshape(q, q, lanes), axis=0)
        add_a = jnp.sum(jnp.where(from_y, adds, 0.0).reshape(q, q, lanes), axis=1)
        hits = jnp.zeros((node_rows, lanes), F32)
        for b in range(q):
            hits = hits + (pick_a[b : b + 1].astype(jnp.int32) == node).astype(F32)
        inverse = 1.0 / jnp.maximum(jnp.sum(hits, axis=1, keepdims=True), 1.0)
        for pick, meta in ((pick_a, meta_a), (pick_b, meta_b)):
            for b in range(q):
                row = pick[b : b + 1]
                meta[b, r : r + 1, :] = row
                meta[b, rels + r : rels + r + 1, :] = jnp.sum(
                    jnp.where(row.astype(jnp.int32) == node, inverse, 0.0), axis=0, keepdims=True
                )
        for b in range(q):
            meta_a[b, 2 * rels + r : 2 * rels + r + 1, :] = add_a[b : b + 1]
    loads[3].wait()

    pl.semaphore_wait(barrier, 2 * (q - 1) + groups - 1)
    start(
        ("z", META, lambda j: meta_a.at[j], lambda t: meta_in_a.at[t]),
        ("y", META + 1, lambda j: meta_b.at[j], lambda t: meta_in_b.at[t]),
    )
    own = pl.ds(pl.multiple_of(core * (node_rows // 2), node_rows // 2), node_rows // 2)
    start(
        ("z", RAW, lambda j: grad.at[own, low], lambda t: raw_a.at[t, own]),
        ("y", RAW + 1, lambda j: grad.at[own, high], lambda t: raw_b.at[t, own]),
    )
    meta_in_a[0] = meta_a[z]
    meta_in_b[0] = meta_b[y]
    raw_a[0] = grad[:, low]
    raw_b[0] = grad[:, high]

    loads[4].wait()
    feat_t[...] = feat[...].T
    self_all[...] = dot(feat_t[...], grad[...], ((1,), (0,)))
    self_rows = width // groups
    strip = self_rows // q
    for b in range(q):
        mine = self_all[pl.ds(pl.multiple_of(k * self_rows + b * strip, strip), strip), :]
        self1[b] = jnp.concatenate([mine[:, low], mine[:, high]], axis=0).astype(BF16)
    start(("y", SELF1, lambda j: self1.at[j], lambda t: self1_in.at[t]))
    self1_in[0] = self1[y]
    loads[5].wait()
    own_rows = node_rows // groups
    mine = pl.ds(pl.multiple_of(k * own_rows, own_rows), own_rows)
    self_term[...] = dot(grad[mine, :], self_w[...], ((1,), (1,)))

    def forward(t):
        ends = (("z", RAW, low, raw_a), ("y", RAW + 1, high, raw_b))
        for axis, row, side, raw in ends:
            copy(row, t, grad.at[own, side], raw.at[t, own], along(axis, z if axis == "z" else y)).wait()
            copy(row - RAW + CORE, t, raw.at[t, own], raw.at[t, own], (n, k + 1 - 2 * core)).start()

    def pick(t):
        other = pl.ds(pl.multiple_of((1 - core) * (node_rows // 2), node_rows // 2), node_rows // 2)
        for side, raw, meta, sent, part, me in (
            (0, raw_a, meta_in_a, meta_a, part_a, y), (1, raw_b, meta_in_b, meta_b, part_b, z),
        ):
            if t > 0:
                copy(META + side, t, sent.at[0], meta.at[t], (n, k)).wait()
                copy(CORE + side, t, raw.at[t, own], raw.at[t, other], (n, k)).wait()
            for r in range(rels):
                hot = (meta[t, r : r + 1, :].astype(jnp.int32) == node).astype(BF16)
                factor = jnp.sum(jnp.where(eye, meta[t, rels + r : rels + r + 1, :], 0.0), axis=1, keepdims=True)
                message = (dot(hot, raw[t], ((0,), (0,))) * factor).astype(BF16)
                part[:, r, t] = message.reshape(q, slots, half)

    def landing_a(r, g):
        return lambda t, j=0: last.at[r, t, pl.ds(g * cut, cut), :, low]

    def landing_b(r, g):
        return lambda t, j=0: last.at[r, pl.ds(g * cut, cut), t, :, high]

    def send_part(g):
        for r in range(rels):
            start(
                ("y", PART + 4 * r + 2 * g, lambda j: part_a.at[j, r, pl.ds(g * cut, cut)], landing_a(r, g)),
                ("z", PART + 4 * r + 2 * g + 1, lambda j: part_b.at[j, r, pl.ds(g * cut, cut)], landing_b(r, g)),
            )

    for t in range(q):
        if t > 0:
            forward(t)
        if t > 1 or t == q - 1:
            for done in ([t - 1] if t < q - 1 else [t - 1, t]):
                if done == 0 and q > 2:
                    continue
                pick(done)
                if done == cut - 1:
                    send_part(0)
        elif t == 0 and q > 2:
            pick(0)
    send_part(1)
    for r in range(rels):
        last[r, 0, :, :, low] = part_a[y, r]
        last[r, :, 0, :, high] = part_b[z, r]

    wide = q * lanes
    same_slot = iota((lanes, wide), 0) == (iota((lanes, wide), 1) // lanes) * slots + iota((lanes, wide), 1) % slots
    same_from = iota((q, wide), 0) == (iota((q, wide), 1) // slots) % q
    tgt_send[...] = jnp.zeros_like(tgt_send)
    for r in range(rels):
        copies = dot(meta_in_a[:, 2 * rels + r, :].astype(BF16), same_slot.astype(BF16), ((1,), (0,)))
        row = jnp.sum(jnp.where(same_from, copies, 0.0), axis=0, keepdims=True)
        for b in range(q):
            tgt_send[b, r : r + 1, :] = row[:, b * lanes : (b + 1) * lanes]
    start(("y", TGT, lambda j: tgt_send.at[j], lambda t: tgt_last.at[t]))
    tgt_last[0] = tgt_send[y]

    finish(("y", SELF1, lambda j: self1.at[j], lambda t, j: self1_in.at[t]))
    total = self1_in[0].astype(F32)
    for b in range(1, q):
        total = total + self1_in[b].astype(F32)
    self2[...] = total
    start(("z", SELF2, lambda j: self2, lambda t: self2_in.at[z]))
    self2_in[z] = total

    finish(("y", TGT, lambda j: tgt_send.at[j], lambda t, j: tgt_last.at[t]))
    for r in range(rels):
        for b in range(q):
            one_hot[r, :, b * lanes : (b + 1) * lanes] = (
                tgt_last[b, r : r + 1, :].astype(jnp.int32) == node
            ).astype(BF16)

    finish(("z", SELF2, lambda j: self2, lambda t, j: self2_in.at[j]))
    total = self2_in[0]
    for b in range(1, q):
        total = total + self2_in[b]
    self3[...] = (total * scale).astype(BF16)
    start(("y", SELF3, lambda j: self3, lambda t: self3_in.at[y]))
    self3_in[y] = self3[...]

    strip_rows = width // q
    for r in range(rels):
        for g in range(2):
            finish(
                ("y", PART + 4 * r + 2 * g, lambda j: part_a.at[j, r, pl.ds(g * cut, cut)], landing_a(r, g)),
                ("z", PART + 4 * r + 2 * g + 1, lambda j: part_b.at[j, r, pl.ds(g * cut, cut)], landing_b(r, g)),
            )
        gathered[r] = dot(one_hot[r], last[r].reshape(q * lanes, width), ((1,), (0,))).astype(BF16)
        grads = dot(feat_t[...], gathered[r], ((1,), (0,))).astype(BF16)
        sum1_a[r] = grads[:, low].reshape(q, strip_rows, half)
        sum1_b[r] = grads[:, high].reshape(q, strip_rows, half)
        start(
            ("y", SUM1 + 2 * r, lambda j: sum1_a.at[r, j], lambda t: sum1_in_a.at[r, t]),
            ("z", SUM1 + 2 * r + 1, lambda j: sum1_b.at[r, j], lambda t: sum1_in_b.at[r, t]),
        )
        sum1_in_a[r, 0] = sum1_a[r, y]
        sum1_in_b[r, 0] = sum1_b[r, z]

    loads[6].wait()
    total = dot(gathered[0], weight[0], ((1,), (1,)))
    for r in range(1, rels):
        total = total + dot(gathered[r], weight[r], ((1,), (1,)))
    share[...] = total.reshape(groups, own_rows, width)
    start(("rel", FEAT, lambda j: share.at[j], lambda t: share_in.at[t]))
    share_in[0] = share[k]

    small = strip_rows // q
    for r in range(rels):
        for axis, s, other, me, sums, sums_in, sends, sends_in in (
            ("y", 0, "z", z, sum1_a, sum1_in_a, sum2_a, sum2_in_a),
            ("z", 1, "y", y, sum1_b, sum1_in_b, sum2_b, sum2_in_b),
        ):
            finish((axis, SUM1 + 2 * r + s, lambda j: sums.at[r, j], lambda t, j: sums_in.at[r, t]))
            total = sums_in[r, 0].astype(F32)
            for b in range(1, q):
                total = total + sums_in[r, b].astype(F32)
            sends[r] = total.reshape(q, small, half)
            start((other, SUM2 + 2 * r + s, lambda j: sends.at[r, j], lambda t: sends_in.at[r, t]))
            sends_in[r, 0] = sends[r, me]
    for r in range(rels):
        for axis, s, me, sends, sends_in, block in (
            ("z", 0, z, sum2_a, sum2_in_a, block_a), ("y", 1, y, sum2_b, sum2_in_b, block_b),
        ):
            finish((axis, SUM2 + 2 * r + s, lambda j: sends.at[r, j], lambda t, j: sends_in.at[r, t]))
            total = sends_in[r, 0]
            for b in range(1, q):
                total = total + sends_in[r, b]
            block[r, me] = total * scale
            start((axis, ALL1 + 2 * r + s, lambda j: block.at[r, me], lambda t: block.at[r, me]))

    def place_of(r, j):
        return pl.ds(pl.multiple_of(r * width + j * strip_rows, strip_rows), strip_rows)

    for r in range(rels):
        for axis, s, me, other, you, block, whole, side in (
            ("z", 0, z, "y", y, block_a, all_a, low), ("y", 1, y, "z", z, block_b, all_b, high),
        ):
            finish((axis, ALL1 + 2 * r + s, lambda j: block.at[r, me], lambda t, j: block.at[r, j]))
            whole[r] = block[r].reshape(strip_rows, half).astype(BF16)
            start((other, ALL2 + 2 * r + s, lambda j: whole.at[r], lambda t: out_rel.at[place_of(r, you), side]))
            out_rel[place_of(r, you), side] = whole[r]

    finish(("rel", FEAT, lambda j: share.at[j], lambda t, j: share_in.at[t]))
    total = self_term[...]
    for b in range(groups):
        total = total + share_in[b]
    out_feat[...] = total.astype(BF16)

    finish(("y", SELF3, lambda j: self3, lambda t, j: self3_in.at[j]))
    for b in range(0, q, 2):
        pair = [self3_in[b + i].astype(F32) for i in (0, 1)]
        wide_rows = [jnp.concatenate([p[:strip], p[strip:]], axis=1) for p in pair]
        out_self[b * strip : (b + 2) * strip, :] = jnp.concatenate(wide_rows, axis=0).astype(BF16)

    for r in range(rels):
        finish(
            ("y", ALL2 + 2 * r, lambda j: all_a.at[r], lambda t, j: out_rel.at[place_of(r, j), low]),
            ("z", ALL2 + 2 * r + 1, lambda j: all_b.at[r], lambda t, j: out_rel.at[place_of(r, j), high]),
        )


def solution(mesh):
    q = int(round(mesh.shape["nodes"] ** 0.5))
    groups = mesh.shape["rel"]

    def per_device(grad_out, node_feats, rel_weight, self_weight, send_rows, recv_rows, send_counts):
        node_rows, width = grad_out.shape
        rels = rel_weight.shape[0]
        slots = send_rows.shape[3]
        half, lanes = width // 2, q * slots
        strip_rows = width // q
        small = strip_rows // q
        strip = width // groups // q
        own_rows = node_rows // groups
        blocks = q * q
        in_hbm = pl.BlockSpec(memory_space=pl.ANY)
        in_vmem = pl.BlockSpec(memory_space=pltpu.VMEM)
        flops = 2 * width * (3 * rels * node_rows * q * lanes + 3 * rels * node_rows * width)

        def two(shape, dtype):
            return [pltpu.VMEM(shape, dtype)] * 2

        outs = pl.pallas_call(
            functools.partial(kernel, q, groups, (node_rows * q * q) ** (-0.5)),
            out_shape=(
                jax.ShapeDtypeStruct((own_rows, width), BF16),
                jax.ShapeDtypeStruct((rels * width, width), BF16),
                jax.ShapeDtypeStruct((width // groups, width), BF16),
            ),
            in_specs=[in_hbm] * 7,
            out_specs=(in_vmem,) * 3,
            scratch_shapes=[
                pltpu.VMEM((node_rows, width), BF16),
                pltpu.VMEM((node_rows, width), BF16),
                pltpu.VMEM((rels, width, width), BF16),
                pltpu.VMEM((width, width), BF16),
                pltpu.VMEM((rels, blocks, slots), jnp.int32),
                pltpu.VMEM((rels, blocks, slots), jnp.int32),
                pltpu.VMEM((rels, 1, blocks), jnp.int32),
            ]
            + two((q, 8, lanes), F32)
            + two((q, 8, lanes), F32)
            + two((q, node_rows, half), BF16)
            + two((q, rels, q, slots, half), BF16)
            + [pltpu.VMEM((rels, q, q, slots, width), BF16)]
            + two((q, 8, lanes), F32)
            + [
                pltpu.VMEM((rels, node_rows, q * lanes), BF16),
                pltpu.VMEM((width, node_rows), BF16),
                pltpu.VMEM((rels, node_rows, width), BF16),
                pltpu.VMEM((width, width), F32),
                pltpu.VMEM((q, 2 * strip, half), BF16),
                pltpu.VMEM((q, 2 * strip, half), BF16),
                pltpu.VMEM((2 * strip, half), F32),
                pltpu.VMEM((q, 2 * strip, half), F32),
                pltpu.VMEM((2 * strip, half), BF16),
                pltpu.VMEM((q, 2 * strip, half), BF16),
                pltpu.VMEM((own_rows, width), F32),
            ]
            + two((groups, own_rows, width), F32)
            + two((rels, q, strip_rows, half), BF16)
            + two((rels, q, strip_rows, half), BF16)
            + two((rels, q, small, half), F32)
            + two((rels, q, small, half), F32)
            + two((rels, q, small, half), F32)
            + two((rels, strip_rows, half), BF16)
            + [
                pltpu.SemaphoreType.DMA((EXCHANGES, max(q, groups))),
                pltpu.SemaphoreType.DMA((EXCHANGES, max(q, groups))),
                pltpu.SemaphoreType.DMA((7,)),
            ],
            compiler_params=pltpu.CompilerParams(
                collective_id=0, has_side_effects=True, vmem_limit_bytes=48 * 1024 * 1024
            ),
            cost_estimate=pl.CostEstimate(flops=flops, bytes_accessed=4 * 1024 * 1024, transcendentals=0),
        )(
            grad_out, node_feats, rel_weight, self_weight,
            send_rows.reshape(rels, blocks, slots), recv_rows.reshape(rels, blocks, slots), send_counts,
        )
        return outs[0], outs[1].reshape(rels, width, width), outs[2]

    return jax.shard_map(
        per_device,
        mesh=mesh,
        in_specs=(
            P("nodes", None),
            P("nodes", None),
            P("rel", None, None),
            P(),
            P("rel", "nodes", None, None),
            P("rel", "nodes", None, None),
            P("rel", "nodes", None),
        ),
        out_specs=(P(("nodes", "rel"), None), P("rel", None, None), P("rel", None)),
        check_vma=False,
    )
```

```python
import functools

import jax
import jax.numpy as jnp
from jax import lax
from jax.experimental import pallas as pl
from jax.experimental.pallas import tpu as pltpu
from jax.sharding import PartitionSpec as P

MESH = pl.DeviceIdType.MESH
F32 = jnp.float32
BF16 = jnp.bfloat16

META, RAW, CORE, PART, SUM1, SUM2, ALL1, ALL2, TGT, SELF1, SELF2, SELF3, FEAT = 0, 2, 4, 6, 14, 18, 22, 26, 30, 31, 32, 33, 34
EXCHANGES = 35


def iota(shape, dim):
    return lax.broadcasted_iota(jnp.int32, shape, dim)


def dot(a, b, contract):
    return lax.dot_general(a, b, ((contract[0], contract[1]), ((), ())), preferred_element_type=F32)


def kernel(
    q, groups, scale,
    grad_hbm, feat_hbm, weight_hbm, self_hbm, rows_hbm, targets_hbm, counts_hbm,
    out_feat, out_rel, out_self,
    grad, feat, weight, self_w, rows, targets, counts,
    meta_a, meta_b, meta_in_a, meta_in_b, raw_a, raw_b, part_a, part_b, last,
    tgt_send, tgt_last, one_hot, feat_t, gathered, self_all, self1, self1_in, self2, self2_in, self3, self3_in,
    self_term, share, share_in, sum1_a, sum1_b, sum1_in_a, sum1_in_b, sum2_a, sum2_b, sum2_in_a, sum2_in_b,
    block_a, block_b, all_a, all_b,
    send_sem, recv_sem, load_sem,
):
    rels, node_rows, width = gathered.shape
    slots = last.shape[3]
    half, lanes, cut = width // 2, q * slots, q // 2
    n = lax.axis_index("nodes")
    k = lax.axis_index("rel")
    z, y, core = n // q, n % q, k % 2
    low, high = slice(0, half), slice(half, width)

    loads = [
        pltpu.make_async_copy(source, target, load_sem.at[i])
        for i, (source, target) in enumerate((
            (rows_hbm, rows), (counts_hbm, counts), (targets_hbm, targets), (grad_hbm, grad),
            (feat_hbm, feat), (self_hbm, self_w), (weight_hbm, weight),
        ))
    ]
    for load in loads:
        load.start()

    def offset(t, count):
        near = (t + 1) // 2
        return (t % 2) * near + (1 - t % 2) * (count - near)

    def along(axis, j):
        return (j * q + y, k) if axis == "z" else ((z * q + j, k) if axis == "y" else (n, j))

    def place(axis):
        return (z, q) if axis == "z" else ((y, q) if axis == "y" else (k, groups))

    def copy(row, t, source, target, device):
        return pltpu.make_async_remote_copy(
            src_ref=source, dst_ref=target, send_sem=send_sem.at[row, t], recv_sem=recv_sem.at[row, t],
            device_id=device, device_id_type=MESH,
        )

    def start(*items, first=1, stop=None):
        def body(t, carry):
            for axis, row, source, target in items:
                me, count = place(axis)
                peer = (me + offset(t, count)) % count
                copy(row, t, source(peer), target(t), along(axis, peer)).start()
            return carry

        lax.fori_loop(first, stop or place(items[0][0])[1], body, 0)

    def finish(*items):
        def body(t, carry):
            for axis, row, source, landing in items:
                me, count = place(axis)
                peer = (me + count - offset(t, count)) % count
                copy(row, t, source(peer), landing(t, peer), along(axis, peer)).wait()
            return carry

        lax.fori_loop(1, place(items[0][0])[1], body, 0)

    barrier = pltpu.get_barrier_semaphore()
    for axis in ("z", "y", "rel"):
        me, count = place(axis)

        def greet(t, carry, axis=axis, me=me, count=count):
            pl.semaphore_signal(barrier, inc=1, device_id=along(axis, (me + t) % count), device_id_type=MESH)
            return carry

        lax.fori_loop(1, count, greet, 0)

    node = iota((node_rows, lanes), 0)
    eye = iota((lanes, lanes), 0) == iota((lanes, lanes), 1)
    blocks = q * q
    spread = (iota((slots, lanes), 0) == iota((slots, lanes), 1) % slots).astype(BF16)
    from_z = iota((blocks, lanes), 0) // q == iota((blocks, lanes), 1) // slots
    from_y = iota((blocks, lanes), 0) % q == iota((blocks, lanes), 1) // slots
    block_eye = iota((blocks, blocks), 0) == iota((blocks, blocks), 1)
    meta_a[...] = jnp.zeros_like(meta_a)
    meta_b[...] = jnp.zeros_like(meta_b)
    for load in loads[:3]:
        load.wait()
    for r in range(rels):
        count = jnp.sum(jnp.where(block_eye, counts[r], 0), axis=1, keepdims=True)
        live = iota((blocks, slots), 1) < count
        picks = dot(jnp.where(live, rows[r], -1).astype(F32).astype(BF16), spread, ((1,), (0,)))
        adds = dot(jnp.where(live, targets[r], -1).astype(F32).astype(BF16), spread, ((1,), (0,)))
        pick_a = jnp.sum(jnp.where(from_y, picks, 0.0).reshape(q, q, lanes), axis=1)
        pick_b = jnp.sum(jnp.where(from_z, picks, 0.0).reshape(q, q, lanes), axis=0)
        add_a = jnp.sum(jnp.where(from_y, adds, 0.0).reshape(q, q, lanes), axis=1)
        hits = jnp.zeros((node_rows, lanes), F32)
        for b in range(q):
            hits = hits + (pick_a[b : b + 1].astype(jnp.int32) == node).astype(F32)
        inverse = 1.0 / jnp.maximum(jnp.sum(hits, axis=1, keepdims=True), 1.0)
        for pick, meta in ((pick_a, meta_a), (pick_b, meta_b)):
            for b in range(q):
                row = pick[b : b + 1]
                meta[b, r : r + 1, :] = row
                meta[b, rels + r : rels + r + 1, :] = jnp.sum(
                    jnp.where(row.astype(jnp.int32) == node, inverse, 0.0), axis=0, keepdims=True
                )
        for b in range(q):
            meta_a[b, 2 * rels + r : 2 * rels + r + 1, :] = add_a[b : b + 1]
    loads[3].wait()

    pl.semaphore_wait(barrier, 2 * (q - 1) + groups - 1)
    own = pl.ds(pl.multiple_of(core * (node_rows // 2), node_rows // 2), node_rows // 2)
    raw_items = (
        ("z", RAW, lambda j: grad.at[own, low], lambda t: raw_a.at[t, own]),
        ("y", RAW + 1, lambda j: grad.at[own, high], lambda t: raw_b.at[t, own]),
    )
    near = min(3, q)
    start(*raw_items, stop=near)
    start(
        ("z", META, lambda j: meta_a.at[j], lambda t: meta_in_a.at[t]),
        ("y", META + 1, lambda j: meta_b.at[j], lambda t: meta_in_b.at[t]),
    )
    if near < q:
        start(*raw_items, first=near)
    meta_in_a[0] = meta_a[z]
    meta_in_b[0] = meta_b[y]
    raw_a[0] = grad[:, low]
    raw_b[0] = grad[:, high]

    loads[4].wait()
    feat_t[...] = feat[...].T
    self_all[...] = dot(feat_t[...], grad[...], ((1,), (0,)))
    self_rows = width // groups
    strip = self_rows // q
    for b in range(q):
        mine = self_all[pl.ds(pl.multiple_of(k * self_rows + b * strip, strip), strip), :]
        self1[b] = jnp.concatenate([mine[:, low], mine[:, high]], axis=0).astype(BF16)
    self1_in[0] = self1[y]
    loads[5].wait()
    own_rows = node_rows // groups
    mine = pl.ds(pl.multiple_of(k * own_rows, own_rows), own_rows)
    self_term[...] = dot(grad[mine, :], self_w[...], ((1,), (1,)))

    finish(
        ("z", META, lambda j: meta_a.at[j], lambda t, j: meta_in_a.at[t]),
        ("y", META + 1, lambda j: meta_b.at[j], lambda t, j: meta_in_b.at[t]),
    )
    wide = q * lanes
    same_slot = iota((lanes, wide), 0) == (iota((lanes, wide), 1) // lanes) * slots + iota((lanes, wide), 1) % slots
    same_from = iota((q, wide), 0) == (iota((q, wide), 1) // slots) % q
    tgt_send[...] = jnp.zeros_like(tgt_send)
    for r in range(rels):
        copies = dot(meta_in_a[:, 2 * rels + r, :].astype(BF16), same_slot.astype(BF16), ((1,), (0,)))
        row = jnp.sum(jnp.where(same_from, copies, 0.0), axis=0, keepdims=True)
        for b in range(q):
            tgt_send[b, r : r + 1, :] = row[:, b * lanes : (b + 1) * lanes]
    start(("y", TGT, lambda j: tgt_send.at[j], lambda t: tgt_last.at[t]))
    tgt_last[0] = tgt_send[y]
    start(("y", SELF1, lambda j: self1.at[j], lambda t: self1_in.at[t]))

    def forward(t):
        ends = (("z", RAW, low, raw_a), ("y", RAW + 1, high, raw_b))
        for axis, row, side, raw in ends:
            copy(row, t, grad.at[own, side], raw.at[t, own], along(axis, z if axis == "z" else y)).wait()
            copy(row - RAW + CORE, t, raw.at[t, own], raw.at[t, own], (n, k + 1 - 2 * core)).start()

    def pick(t):
        other = pl.ds(pl.multiple_of((1 - core) * (node_rows // 2), node_rows // 2), node_rows // 2)
        for side, raw, meta, part in ((0, raw_a, meta_in_a, part_a), (1, raw_b, meta_in_b, part_b)):
            if t > 0:
                copy(CORE + side, t, raw.at[t, own], raw.at[t, other], (n, k)).wait()
            for r in range(rels):
                hot = (meta[t, r : r + 1, :].astype(jnp.int32) == node).astype(BF16)
                factor = jnp.sum(jnp.where(eye, meta[t, rels + r : rels + r + 1, :], 0.0), axis=1, keepdims=True)
                message = (dot(hot, raw[t], ((0,), (0,))) * factor).astype(BF16)
                part[:, r, t] = message.reshape(q, slots, half)

    def landing_a(r, g):
        return lambda t, j=0: last.at[r, t, pl.ds(g * cut, cut), :, low]

    def landing_b(r, g):
        return lambda t, j=0: last.at[r, pl.ds(g * cut, cut), t, :, high]

    def send_part(g):
        for r in range(rels):
            start(
                ("y", PART + 4 * r + 2 * g, lambda j: part_a.at[j, r, pl.ds(g * cut, cut)], landing_a(r, g)),
                ("z", PART + 4 * r + 2 * g + 1, lambda j: part_b.at[j, r, pl.ds(g * cut, cut)], landing_b(r, g)),
            )

    for t in range(q):
        if t > 0:
            forward(t)
        if t > 1 or t == q - 1:
            for done in ([t - 1] if t < q - 1 else [t - 1, t]):
                if done == 0 and q > 2:
                    continue
                pick(done)
                if done == cut - 1:
                    send_part(0)
        elif t == 0 and q > 2:
            pick(0)
    finish(("y", SELF1, lambda j: self1.at[j], lambda t, j: self1_in.at[t]))
    total = self1_in[0].astype(F32)
    for b in range(1, q):
        total = total + self1_in[b].astype(F32)
    self2[...] = total
    start(("z", SELF2, lambda j: self2, lambda t: self2_in.at[z]))
    self2_in[z] = total

    send_part(1)
    for r in range(rels):
        last[r, 0, :, :, low] = part_a[y, r]
        last[r, :, 0, :, high] = part_b[z, r]

    finish(("y", TGT, lambda j: tgt_send.at[j], lambda t, j: tgt_last.at[t]))
    for r in range(rels):
        for b in range(q):
            one_hot[r, :, b * lanes : (b + 1) * lanes] = (
                tgt_last[b, r : r + 1, :].astype(jnp.int32) == node
            ).astype(BF16)

    finish(("z", SELF2, lambda j: self2, lambda t, j: self2_in.at[j]))
    total = self2_in[0]
    for b in range(1, q):
        total = total + self2_in[b]
    self3[...] = (total * scale).astype(BF16)
    start(("y", SELF3, lambda j: self3, lambda t: self3_in.at[y]))
    self3_in[y] = self3[...]

    strip_rows = width // q
    for r in range(rels):
        for g in range(2):
            finish(
                ("y", PART + 4 * r + 2 * g, lambda j: part_a.at[j, r, pl.ds(g * cut, cut)], landing_a(r, g)),
                ("z", PART + 4 * r + 2 * g + 1, lambda j: part_b.at[j, r, pl.ds(g * cut, cut)], landing_b(r, g)),
            )
        gathered[r] = dot(one_hot[r], last[r].reshape(q * lanes, width), ((1,), (0,))).astype(BF16)
        grads = dot(feat_t[...], gathered[r], ((1,), (0,))).astype(BF16)
        sum1_a[r] = grads[:, low].reshape(q, strip_rows, half)
        sum1_b[r] = grads[:, high].reshape(q, strip_rows, half)
        start(
            ("y", SUM1 + 2 * r, lambda j: sum1_a.at[r, j], lambda t: sum1_in_a.at[r, t]),
            ("z", SUM1 + 2 * r + 1, lambda j: sum1_b.at[r, j], lambda t: sum1_in_b.at[r, t]),
        )
        sum1_in_a[r, 0] = sum1_a[r, y]
        sum1_in_b[r, 0] = sum1_b[r, z]

    loads[6].wait()
    total = dot(gathered[0], weight[0], ((1,), (1,)))
    for r in range(1, rels):
        total = total + dot(gathered[r], weight[r], ((1,), (1,)))
    share[...] = total.reshape(groups, own_rows, width)
    start(("rel", FEAT, lambda j: share.at[j], lambda t: share_in.at[t]))
    share_in[0] = share[k]

    small = strip_rows // q
    for r in range(rels):
        for axis, s, other, me, sums, sums_in, sends, sends_in in (
            ("y", 0, "z", z, sum1_a, sum1_in_a, sum2_a, sum2_in_a),
            ("z", 1, "y", y, sum1_b, sum1_in_b, sum2_b, sum2_in_b),
        ):
            finish((axis, SUM1 + 2 * r + s, lambda j: sums.at[r, j], lambda t, j: sums_in.at[r, t]))
            total = sums_in[r, 0].astype(F32)
            for b in range(1, q):
                total = total + sums_in[r, b].astype(F32)
            sends[r] = total.reshape(q, small, half)
            start((other, SUM2 + 2 * r + s, lambda j: sends.at[r, j], lambda t: sends_in.at[r, t]))
            sends_in[r, 0] = sends[r, me]
    for r in range(rels):
        for axis, s, me, sends, sends_in, block in (
            ("z", 0, z, sum2_a, sum2_in_a, block_a), ("y", 1, y, sum2_b, sum2_in_b, block_b),
        ):
            finish((axis, SUM2 + 2 * r + s, lambda j: sends.at[r, j], lambda t, j: sends_in.at[r, t]))
            total = sends_in[r, 0]
            for b in range(1, q):
                total = total + sends_in[r, b]
            total = total * scale
            block[r, me] = jnp.concatenate([total[:, : half // 2], total[:, half // 2 :]], axis=0).astype(BF16)
            start((axis, ALL1 + 2 * r + s, lambda j: block.at[r, me], lambda t: block.at[r, me]))

    def place_of(r, j):
        return pl.ds(pl.multiple_of(r * width + j * strip_rows, strip_rows), strip_rows)

    for r in range(rels):
        for axis, s, me, other, you, block, whole, side in (
            ("z", 0, z, "y", y, block_a, all_a, low), ("y", 1, y, "z", z, block_b, all_b, high),
        ):
            finish((axis, ALL1 + 2 * r + s, lambda j: block.at[r, me], lambda t, j: block.at[r, j]))
            pieces = block[r].astype(F32)
            sides = [pieces[:, i * small : (i + 1) * small, :].reshape(strip_rows, half // 2) for i in (0, 1)]
            whole[r] = jnp.concatenate(sides, axis=1).astype(BF16)
            start((other, ALL2 + 2 * r + s, lambda j: whole.at[r], lambda t: out_rel.at[place_of(r, you), side]))
            out_rel[place_of(r, you), side] = whole[r]

    finish(("rel", FEAT, lambda j: share.at[j], lambda t, j: share_in.at[t]))
    total = self_term[...]
    for b in range(groups):
        total = total + share_in[b]
    out_feat[...] = total.astype(BF16)

    finish(("y", SELF3, lambda j: self3, lambda t, j: self3_in.at[j]))
    for b in range(0, q, 2):
        pair = [self3_in[b + i].astype(F32) for i in (0, 1)]
        wide_rows = [jnp.concatenate([p[:strip], p[strip:]], axis=1) for p in pair]
        out_self[b * strip : (b + 2) * strip, :] = jnp.concatenate(wide_rows, axis=0).astype(BF16)

    for r in range(rels):
        finish(
            ("y", ALL2 + 2 * r, lambda j: all_a.at[r], lambda t, j: out_rel.at[place_of(r, j), low]),
            ("z", ALL2 + 2 * r + 1, lambda j: all_b.at[r], lambda t, j: out_rel.at[place_of(r, j), high]),
        )


def solution(mesh):
    q = int(round(mesh.shape["nodes"] ** 0.5))
    groups = mesh.shape["rel"]

    def per_device(grad_out, node_feats, rel_weight, self_weight, send_rows, recv_rows, send_counts):
        node_rows, width = grad_out.shape
        rels = rel_weight.shape[0]
        slots = send_rows.shape[3]
        half, lanes = width // 2, q * slots
        strip_rows = width // q
        small = strip_rows // q
        strip = width // groups // q
        own_rows = node_rows // groups
        blocks = q * q
        in_hbm = pl.BlockSpec(memory_space=pltpu.HBM)
        in_vmem = pl.BlockSpec(memory_space=pltpu.VMEM)
        flops = 2 * width * (3 * rels * node_rows * q * lanes + 3 * rels * node_rows * width)

        def two(shape, dtype):
            return [pltpu.VMEM(shape, dtype)] * 2

        outs = pl.pallas_call(
            functools.partial(kernel, q, groups, (node_rows * q * q) ** (-0.5)),
            out_shape=(
                jax.ShapeDtypeStruct((own_rows, width), BF16),
                jax.ShapeDtypeStruct((rels * width, width), BF16),
                jax.ShapeDtypeStruct((width // groups, width), BF16),
            ),
            in_specs=[in_hbm] * 7,
            out_specs=(in_vmem,) * 3,
            scratch_shapes=[
                pltpu.VMEM((node_rows, width), BF16),
                pltpu.VMEM((node_rows, width), BF16),
                pltpu.VMEM((rels, width, width), BF16),
                pltpu.VMEM((width, width), BF16),
                pltpu.VMEM((rels, blocks, slots), jnp.int32),
                pltpu.VMEM((rels, blocks, slots), jnp.int32),
                pltpu.VMEM((rels, 1, blocks), jnp.int32),
            ]
            + two((q, 8, lanes), F32)
            + two((q, 8, lanes), F32)
            + two((q, node_rows, half), BF16)
            + two((q, rels, q, slots, half), BF16)
            + [pltpu.VMEM((rels, q, q, slots, width), BF16)]
            + two((q, 8, lanes), F32)
            + [
                pltpu.VMEM((rels, node_rows, q * lanes), BF16),
                pltpu.VMEM((width, node_rows), BF16),
                pltpu.VMEM((rels, node_rows, width), BF16),
                pltpu.VMEM((width, width), F32),
                pltpu.VMEM((q, 2 * strip, half), BF16),
                pltpu.VMEM((q, 2 * strip, half), BF16),
                pltpu.VMEM((2 * strip, half), F32),
                pltpu.VMEM((q, 2 * strip, half), F32),
                pltpu.VMEM((2 * strip, half), BF16),
                pltpu.VMEM((q, 2 * strip, half), BF16),
                pltpu.VMEM((own_rows, width), F32),
            ]
            + two((groups, own_rows, width), F32)
            + two((rels, q, strip_rows, half), BF16)
            + two((rels, q, strip_rows, half), BF16)
            + two((rels, q, small, half), F32)
            + two((rels, q, small, half), F32)
            + two((rels, q, 2 * small, half // 2), BF16)
            + two((rels, strip_rows, half), BF16)
            + [
                pltpu.SemaphoreType.DMA((EXCHANGES, max(q, groups))),
                pltpu.SemaphoreType.DMA((EXCHANGES, max(q, groups))),
                pltpu.SemaphoreType.DMA((7,)),
            ],
            compiler_params=pltpu.CompilerParams(
                collective_id=0, has_side_effects=True, vmem_limit_bytes=48 * 1024 * 1024
            ),
            cost_estimate=pl.CostEstimate(flops=flops, bytes_accessed=4 * 1024 * 1024, transcendentals=0),
        )(
            grad_out, node_feats, rel_weight, self_weight,
            send_rows.reshape(rels, blocks, slots), recv_rows.reshape(rels, blocks, slots), send_counts,
        )
        return outs[0], outs[1].reshape(rels, width, width), outs[2]

    return jax.shard_map(
        per_device,
        mesh=mesh,
        in_specs=(
            P("nodes", None),
            P("nodes", None),
            P("rel", None, None),
            P(),
            P("rel", "nodes", None, None),
            P("rel", "nodes", None, None),
            P("rel", "nodes", None),
        ),
        out_specs=(P(("nodes", "rel"), None), P("rel", None, None), P("rel", None)),
        check_vma=False,
    )
```

```python
import functools

import jax
import jax.numpy as jnp
from jax import lax
from jax.experimental import pallas as pl
from jax.experimental.pallas import tpu as pltpu
from jax.sharding import PartitionSpec as P

MESH = pl.DeviceIdType.MESH
F32 = jnp.float32
BF16 = jnp.bfloat16

META, RAW, CORE, PART, SUM1, SUM2, ALL1, ALL2, TGT, SELF1, SELF2, SELF3, FEAT = 0, 2, 4, 6, 14, 18, 22, 26, 30, 31, 32, 33, 34
EXCHANGES = 35


def iota(shape, dim):
    return lax.broadcasted_iota(jnp.int32, shape, dim)


def dot(a, b, contract):
    return lax.dot_general(a, b, ((contract[0], contract[1]), ((), ())), preferred_element_type=F32)


def kernel(
    q, groups, scale,
    grad_hbm, feat_hbm, weight_hbm, self_hbm, rows_hbm, targets_hbm, counts_hbm,
    out_feat, out_rel, out_self,
    grad, feat, weight, self_w, rows, targets, counts,
    meta_a, meta_b, meta_in_a, meta_in_b, raw_a, raw_b, part_a, part_b, last,
    tgt_send, tgt_last, one_hot, feat_t, gathered, self_all, self1, self1_in, self2, self2_in, self3, self3_in,
    self_term, share, share_in, sum1_a, sum1_b, sum1_in_a, sum1_in_b, sum2_a, sum2_b, sum2_in_a, sum2_in_b,
    block_a, block_b, all_a, all_b, feat_out, self_out,
    send_sem, recv_sem, load_sem, store_sem,
):
    rels, node_rows, width = gathered.shape
    slots = last.shape[3]
    half, lanes, cut = width // 2, q * slots, q // 2
    n = lax.axis_index("nodes")
    k = lax.axis_index("rel")
    z, y, core = n // q, n % q, k % 2
    low, high = slice(0, half), slice(half, width)

    loads = [
        pltpu.make_async_copy(source, target, load_sem.at[i])
        for i, (source, target) in enumerate((
            (rows_hbm, rows), (counts_hbm, counts), (targets_hbm, targets), (grad_hbm, grad),
            (feat_hbm, feat), (self_hbm, self_w), (weight_hbm, weight),
        ))
    ]
    for load in loads:
        load.start()

    def offset(t, count):
        near = (t + 1) // 2
        return (t % 2) * near + (1 - t % 2) * (count - near)

    def along(axis, j):
        return (j * q + y, k) if axis == "z" else ((z * q + j, k) if axis == "y" else (n, j))

    def place(axis):
        return (z, q) if axis == "z" else ((y, q) if axis == "y" else (k, groups))

    def copy(row, t, source, target, device):
        return pltpu.make_async_remote_copy(
            src_ref=source, dst_ref=target, send_sem=send_sem.at[row, t], recv_sem=recv_sem.at[row, t],
            device_id=device, device_id_type=MESH,
        )

    def start(*items, first=1, stop=None):
        def body(t, carry):
            for axis, row, source, target in items:
                me, count = place(axis)
                peer = (me + offset(t, count)) % count
                copy(row, t, source(peer), target(t), along(axis, peer)).start()
            return carry

        lax.fori_loop(first, stop or place(items[0][0])[1], body, 0)

    def finish(*items):
        def body(t, carry):
            for axis, row, source, landing in items:
                me, count = place(axis)
                peer = (me + count - offset(t, count)) % count
                copy(row, t, source(peer), landing(t, peer), along(axis, peer)).wait()
            return carry

        lax.fori_loop(1, place(items[0][0])[1], body, 0)

    barrier = pltpu.get_barrier_semaphore()
    for axis in ("z", "y", "rel"):
        me, count = place(axis)

        def greet(t, carry, axis=axis, me=me, count=count):
            pl.semaphore_signal(barrier, inc=1, device_id=along(axis, (me + t) % count), device_id_type=MESH)
            return carry

        lax.fori_loop(1, count, greet, 0)

    node = iota((node_rows, lanes), 0)
    eye = iota((lanes, lanes), 0) == iota((lanes, lanes), 1)
    blocks = q * q
    spread = (iota((slots, lanes), 0) == iota((slots, lanes), 1) % slots).astype(BF16)
    from_z = iota((blocks, lanes), 0) // q == iota((blocks, lanes), 1) // slots
    from_y = iota((blocks, lanes), 0) % q == iota((blocks, lanes), 1) // slots
    meta_a[...] = jnp.zeros_like(meta_a)
    meta_b[...] = jnp.zeros_like(meta_b)
    for load in loads[:3]:
        load.wait()
    for r in range(rels):
        live = iota((slots, blocks), 0) < counts[r]
        picks = dot(jnp.where(live, rows[r], -1).astype(F32).astype(BF16), spread, ((0,), (0,)))
        adds = dot(jnp.where(live, targets[r], -1).astype(F32).astype(BF16), spread, ((0,), (0,)))
        pick_a = jnp.sum(jnp.where(from_y, picks, 0.0).reshape(q, q, lanes), axis=1)
        pick_b = jnp.sum(jnp.where(from_z, picks, 0.0).reshape(q, q, lanes), axis=0)
        add_a = jnp.sum(jnp.where(from_y, adds, 0.0).reshape(q, q, lanes), axis=1)
        hits = jnp.zeros((node_rows, lanes), F32)
        for b in range(q):
            hits = hits + (pick_a[b : b + 1].astype(jnp.int32) == node).astype(F32)
        inverse = 1.0 / jnp.maximum(jnp.sum(hits, axis=1, keepdims=True), 1.0)
        for pick, meta in ((pick_a, meta_a), (pick_b, meta_b)):
            for b in range(q):
                row = pick[b : b + 1]
                meta[b, r : r + 1, :] = row
                meta[b, rels + r : rels + r + 1, :] = jnp.sum(
                    jnp.where(row.astype(jnp.int32) == node, inverse, 0.0), axis=0, keepdims=True
                )
        for b in range(q):
            meta_a[b, 2 * rels + r : 2 * rels + r + 1, :] = add_a[b : b + 1]
    loads[3].wait()

    pl.semaphore_wait(barrier, 2 * (q - 1) + groups - 1)
    own = pl.ds(pl.multiple_of(core * (node_rows // 2), node_rows // 2), node_rows // 2)
    raw_items = (
        ("z", RAW, lambda j: grad.at[own, low], lambda t: raw_a.at[t, own]),
        ("y", RAW + 1, lambda j: grad.at[own, high], lambda t: raw_b.at[t, own]),
    )
    near = min(3, q)
    start(*raw_items, stop=near)
    start(
        ("z", META, lambda j: meta_a.at[j], lambda t: meta_in_a.at[t]),
        ("y", META + 1, lambda j: meta_b.at[j], lambda t: meta_in_b.at[t]),
    )
    if near < q:
        start(*raw_items, first=near)
    meta_in_a[0] = meta_a[z]
    meta_in_b[0] = meta_b[y]
    raw_a[0] = grad[:, low]
    raw_b[0] = grad[:, high]

    loads[4].wait()
    feat_t[...] = feat[...].T
    self_all[...] = dot(feat_t[...], grad[...], ((1,), (0,)))
    self_rows = width // groups
    strip = self_rows // q
    for b in range(q):
        mine = self_all[pl.ds(pl.multiple_of(k * self_rows + b * strip, strip), strip), :]
        self1[b] = jnp.concatenate([mine[:, low], mine[:, high]], axis=0).astype(BF16)
    self1_in[0] = self1[y]
    loads[5].wait()
    own_rows = node_rows // groups
    mine = pl.ds(pl.multiple_of(k * own_rows, own_rows), own_rows)
    self_term[...] = dot(grad[mine, :], self_w[...], ((1,), (1,)))

    finish(
        ("z", META, lambda j: meta_a.at[j], lambda t, j: meta_in_a.at[t]),
        ("y", META + 1, lambda j: meta_b.at[j], lambda t, j: meta_in_b.at[t]),
    )
    wide = q * lanes
    same_slot = iota((lanes, wide), 0) == (iota((lanes, wide), 1) // lanes) * slots + iota((lanes, wide), 1) % slots
    same_from = iota((q, wide), 0) == (iota((q, wide), 1) // slots) % q
    tgt_send[...] = jnp.zeros_like(tgt_send)
    for r in range(rels):
        copies = dot(meta_in_a[:, 2 * rels + r, :].astype(BF16), same_slot.astype(BF16), ((1,), (0,)))
        row = jnp.sum(jnp.where(same_from, copies, 0.0), axis=0, keepdims=True)
        for b in range(q):
            tgt_send[b, r : r + 1, :] = row[:, b * lanes : (b + 1) * lanes]
    start(("y", TGT, lambda j: tgt_send.at[j], lambda t: tgt_last.at[t]))
    tgt_last[0] = tgt_send[y]
    start(("y", SELF1, lambda j: self1.at[j], lambda t: self1_in.at[t]))

    def forward(t):
        ends = (("z", RAW, low, raw_a), ("y", RAW + 1, high, raw_b))
        for axis, row, side, raw in ends:
            copy(row, t, grad.at[own, side], raw.at[t, own], along(axis, z if axis == "z" else y)).wait()
            copy(row - RAW + CORE, t, raw.at[t, own], raw.at[t, own], (n, k + 1 - 2 * core)).start()

    def pick(t):
        other = pl.ds(pl.multiple_of((1 - core) * (node_rows // 2), node_rows // 2), node_rows // 2)
        for side, raw, meta, part in ((0, raw_a, meta_in_a, part_a), (1, raw_b, meta_in_b, part_b)):
            if t > 0:
                copy(CORE + side, t, raw.at[t, own], raw.at[t, other], (n, k)).wait()
            for r in range(rels):
                hot = (meta[t, r : r + 1, :].astype(jnp.int32) == node).astype(BF16)
                factor = jnp.sum(jnp.where(eye, meta[t, rels + r : rels + r + 1, :], 0.0), axis=1, keepdims=True)
                message = (dot(hot, raw[t], ((0,), (0,))) * factor).astype(BF16)
                part[:, r, t] = message.reshape(q, slots, half)

    def landing_a(r, g):
        return lambda t, j=0: last.at[r, t, pl.ds(g * cut, cut), :, low]

    def landing_b(r, g):
        return lambda t, j=0: last.at[r, pl.ds(g * cut, cut), t, :, high]

    def send_part(g):
        for r in range(rels):
            start(
                ("y", PART + 4 * r + 2 * g, lambda j: part_a.at[j, r, pl.ds(g * cut, cut)], landing_a(r, g)),
                ("z", PART + 4 * r + 2 * g + 1, lambda j: part_b.at[j, r, pl.ds(g * cut, cut)], landing_b(r, g)),
            )

    for t in range(q):
        if t > 0:
            forward(t)
        if t > 1 or t == q - 1:
            for done in ([t - 1] if t < q - 1 else [t - 1, t]):
                if done == 0 and q > 2:
                    continue
                pick(done)
                if done == cut - 1:
                    send_part(0)
        elif t == 0 and q > 2:
            pick(0)
    finish(("y", SELF1, lambda j: self1.at[j], lambda t, j: self1_in.at[t]))
    total = self1_in[0].astype(F32)
    for b in range(1, q):
        total = total + self1_in[b].astype(F32)
    self2[...] = total
    start(("z", SELF2, lambda j: self2, lambda t: self2_in.at[z]))
    self2_in[z] = total

    send_part(1)
    for r in range(rels):
        last[r, 0, :, :, low] = part_a[y, r]
        last[r, :, 0, :, high] = part_b[z, r]

    finish(("y", TGT, lambda j: tgt_send.at[j], lambda t, j: tgt_last.at[t]))
    for r in range(rels):
        for b in range(q):
            one_hot[r, :, b * lanes : (b + 1) * lanes] = (
                tgt_last[b, r : r + 1, :].astype(jnp.int32) == node
            ).astype(BF16)

    finish(("z", SELF2, lambda j: self2, lambda t, j: self2_in.at[j]))
    total = self2_in[0]
    for b in range(1, q):
        total = total + self2_in[b]
    self3[...] = (total * scale).astype(BF16)
    start(("y", SELF3, lambda j: self3, lambda t: self3_in.at[y]))
    self3_in[y] = self3[...]

    strip_rows = width // q
    for r in range(rels):
        for g in range(2):
            finish(
                ("y", PART + 4 * r + 2 * g, lambda j: part_a.at[j, r, pl.ds(g * cut, cut)], landing_a(r, g)),
                ("z", PART + 4 * r + 2 * g + 1, lambda j: part_b.at[j, r, pl.ds(g * cut, cut)], landing_b(r, g)),
            )
        gathered[r] = dot(one_hot[r], last[r].reshape(q * lanes, width), ((1,), (0,))).astype(BF16)
        grads = dot(feat_t[...], gathered[r], ((1,), (0,))).astype(BF16)
        sum1_a[r] = grads[:, low].reshape(q, strip_rows, half)
        sum1_b[r] = grads[:, high].reshape(q, strip_rows, half)
        start(
            ("y", SUM1 + 2 * r, lambda j: sum1_a.at[r, j], lambda t: sum1_in_a.at[r, t]),
            ("z", SUM1 + 2 * r + 1, lambda j: sum1_b.at[r, j], lambda t: sum1_in_b.at[r, t]),
        )
        sum1_in_a[r, 0] = sum1_a[r, y]
        sum1_in_b[r, 0] = sum1_b[r, z]

    loads[6].wait()
    total = dot(gathered[0], weight[0], ((1,), (1,)))
    for r in range(1, rels):
        total = total + dot(gathered[r], weight[r], ((1,), (1,)))
    share[...] = total.reshape(groups, own_rows, width)
    start(("rel", FEAT, lambda j: share.at[j], lambda t: share_in.at[t]))
    share_in[0] = share[k]

    small = strip_rows // q
    for r in range(rels):
        for axis, s, other, me, sums, sums_in, sends, sends_in in (
            ("y", 0, "z", z, sum1_a, sum1_in_a, sum2_a, sum2_in_a),
            ("z", 1, "y", y, sum1_b, sum1_in_b, sum2_b, sum2_in_b),
        ):
            finish((axis, SUM1 + 2 * r + s, lambda j: sums.at[r, j], lambda t, j: sums_in.at[r, t]))
            total = sums_in[r, 0].astype(F32)
            for b in range(1, q):
                total = total + sums_in[r, b].astype(F32)
            sends[r] = total.reshape(q, small, half)
            start((other, SUM2 + 2 * r + s, lambda j: sends.at[r, j], lambda t: sends_in.at[r, t]))
            sends_in[r, 0] = sends[r, me]
    for r in range(rels):
        for axis, s, me, sends, sends_in, block in (
            ("z", 0, z, sum2_a, sum2_in_a, block_a), ("y", 1, y, sum2_b, sum2_in_b, block_b),
        ):
            finish((axis, SUM2 + 2 * r + s, lambda j: sends.at[r, j], lambda t, j: sends_in.at[r, t]))
            total = sends_in[r, 0]
            for b in range(1, q):
                total = total + sends_in[r, b]
            total = total * scale
            block[r, me] = jnp.concatenate([total[:, : half // 2], total[:, half // 2 :]], axis=0).astype(BF16)
            start((axis, ALL1 + 2 * r + s, lambda j: block.at[r, me], lambda t: block.at[r, me]))

    stores = []

    def place_of(r, j):
        return pl.ds(pl.multiple_of(r * width + j * strip_rows, strip_rows), strip_rows)

    for r in range(rels):
        for axis, s, me, other, you, block, whole, side in (
            ("z", 0, z, "y", y, block_a, all_a, low), ("y", 1, y, "z", z, block_b, all_b, high),
        ):
            finish((axis, ALL1 + 2 * r + s, lambda j: block.at[r, me], lambda t, j: block.at[r, j]))
            pieces = block[r].astype(F32)
            sides = [pieces[:, i * small : (i + 1) * small, :].reshape(strip_rows, half // 2) for i in (0, 1)]
            whole[r] = jnp.concatenate(sides, axis=1).astype(BF16)
            start((other, ALL2 + 2 * r + s, lambda j: whole.at[r], lambda t: out_rel.at[place_of(r, you), side]))
            stores.append(pltpu.make_async_copy(
                whole.at[r], out_rel.at[place_of(r, you), side], store_sem.at[2 + 2 * r + s]
            ))
            stores[-1].start()

    finish(("rel", FEAT, lambda j: share.at[j], lambda t, j: share_in.at[t]))
    total = self_term[...]
    for b in range(groups):
        total = total + share_in[b]
    feat_out[...] = total.astype(BF16)
    stores.append(pltpu.make_async_copy(feat_out, out_feat, store_sem.at[0]))
    stores[-1].start()

    finish(("y", SELF3, lambda j: self3, lambda t, j: self3_in.at[j]))
    for b in range(0, q, 2):
        pair = [self3_in[b + i].astype(F32) for i in (0, 1)]
        wide_rows = [jnp.concatenate([p[:strip], p[strip:]], axis=1) for p in pair]
        self_out[b * strip : (b + 2) * strip, :] = jnp.concatenate(wide_rows, axis=0).astype(BF16)
    stores.append(pltpu.make_async_copy(self_out, out_self, store_sem.at[1]))
    stores[-1].start()

    for r in range(rels):
        finish(
            ("y", ALL2 + 2 * r, lambda j: all_a.at[r], lambda t, j: out_rel.at[place_of(r, j), low]),
            ("z", ALL2 + 2 * r + 1, lambda j: all_b.at[r], lambda t, j: out_rel.at[place_of(r, j), high]),
        )
    for store in stores:
        store.wait()


def solution(mesh):
    q = int(round(mesh.shape["nodes"] ** 0.5))
    groups = mesh.shape["rel"]

    def per_device(grad_out, node_feats, rel_weight, self_weight, send_rows, recv_rows, send_counts):
        node_rows, width = grad_out.shape
        rels = rel_weight.shape[0]
        slots = send_rows.shape[3]
        half, lanes = width // 2, q * slots
        strip_rows = width // q
        small = strip_rows // q
        strip = width // groups // q
        own_rows = node_rows // groups
        blocks = q * q
        in_hbm = pl.BlockSpec(memory_space=pltpu.HBM)
        flops = 2 * width * (3 * rels * node_rows * q * lanes + 3 * rels * node_rows * width)

        def two(shape, dtype):
            return [pltpu.VMEM(shape, dtype)] * 2

        outs = pl.pallas_call(
            functools.partial(kernel, q, groups, (node_rows * q * q) ** (-0.5)),
            out_shape=(
                jax.ShapeDtypeStruct((own_rows, width), BF16),
                jax.ShapeDtypeStruct((rels * width, width), BF16),
                jax.ShapeDtypeStruct((width // groups, width), BF16),
            ),
            in_specs=[in_hbm] * 7,
            out_specs=(in_hbm,) * 3,
            scratch_shapes=[
                pltpu.VMEM((node_rows, width), BF16),
                pltpu.VMEM((node_rows, width), BF16),
                pltpu.VMEM((rels, width, width), BF16),
                pltpu.VMEM((width, width), BF16),
                pltpu.VMEM((rels, slots, blocks), jnp.int32),
                pltpu.VMEM((rels, slots, blocks), jnp.int32),
                pltpu.VMEM((rels, 1, blocks), jnp.int32),
            ]
            + two((q, 8, lanes), F32)
            + two((q, 8, lanes), F32)
            + two((q, node_rows, half), BF16)
            + two((q, rels, q, slots, half), BF16)
            + [pltpu.VMEM((rels, q, q, slots, width), BF16)]
            + two((q, 8, lanes), F32)
            + [
                pltpu.VMEM((rels, node_rows, q * lanes), BF16),
                pltpu.VMEM((width, node_rows), BF16),
                pltpu.VMEM((rels, node_rows, width), BF16),
                pltpu.VMEM((width, width), F32),
                pltpu.VMEM((q, 2 * strip, half), BF16),
                pltpu.VMEM((q, 2 * strip, half), BF16),
                pltpu.VMEM((2 * strip, half), F32),
                pltpu.VMEM((q, 2 * strip, half), F32),
                pltpu.VMEM((2 * strip, half), BF16),
                pltpu.VMEM((q, 2 * strip, half), BF16),
                pltpu.VMEM((own_rows, width), F32),
            ]
            + two((groups, own_rows, width), F32)
            + two((rels, q, strip_rows, half), BF16)
            + two((rels, q, strip_rows, half), BF16)
            + two((rels, q, small, half), F32)
            + two((rels, q, small, half), F32)
            + two((rels, q, 2 * small, half // 2), BF16)
            + two((rels, strip_rows, half), BF16)
            + [
                pltpu.VMEM((own_rows, width), BF16),
                pltpu.VMEM((width // groups, width), BF16),
                pltpu.SemaphoreType.DMA((EXCHANGES, max(q, groups))),
                pltpu.SemaphoreType.DMA((EXCHANGES, max(q, groups))),
                pltpu.SemaphoreType.DMA((7,)),
                pltpu.SemaphoreType.DMA((2 + 2 * rels,)),
            ],
            compiler_params=pltpu.CompilerParams(
                collective_id=0, has_side_effects=True, vmem_limit_bytes=60 * 1024 * 1024
            ),
            cost_estimate=pl.CostEstimate(flops=flops, bytes_accessed=4 * 1024 * 1024, transcendentals=0),
        )(
            grad_out, node_feats, rel_weight, self_weight,
            send_rows.transpose(0, 1, 3, 2).reshape(rels, slots, blocks),
            recv_rows.transpose(0, 1, 3, 2).reshape(rels, slots, blocks),
            send_counts,
        )
        return outs[0], outs[1].reshape(rels, width, width), outs[2]

    return jax.shard_map(
        per_device,
        mesh=mesh,
        in_specs=(
            P("nodes", None),
            P("nodes", None),
            P("rel", None, None),
            P(),
            P("rel", "nodes", None, None),
            P("rel", "nodes", None, None),
            P("rel", "nodes", None),
        ),
        out_specs=(P(("nodes", "rel"), None), P("rel", None, None), P("rel", None)),
        check_vma=False,
    )
```

```python
import functools

import jax
import jax.numpy as jnp
from jax import lax
from jax.experimental import pallas as pl
from jax.experimental.pallas import tpu as pltpu
from jax.sharding import PartitionSpec as P

MESH = pl.DeviceIdType.MESH
F32 = jnp.float32
BF16 = jnp.bfloat16

META, RAW, CORE, PART, SUM1, SUM2, ALL1, ALL2, TGT, SELF1, SELF2, SELF3, FEAT = 0, 2, 4, 6, 16, 20, 24, 28, 32, 33, 34, 35, 36
EXCHANGES = 37


def iota(shape, dim):
    return lax.broadcasted_iota(jnp.int32, shape, dim)


def dot(a, b, contract):
    return lax.dot_general(a, b, ((contract[0], contract[1]), ((), ())), preferred_element_type=F32)


def kernel(
    q, groups, scale,
    grad_hbm, feat_hbm, weight_hbm, self_hbm, rows_hbm, targets_hbm, counts_hbm,
    out_feat, out_rel, out_self,
    grad, feat, weight, self_w, rows, targets, counts,
    meta_a, meta_b, meta_in_a, meta_in_b, raw_a, raw_b, part_a, part_b, last,
    tgt_send, tgt_last, one_hot, feat_t, gathered, self_all, self1, self1_in, self2, self2_in, self3, self3_in,
    self_term, share, share_in, sum1_a, sum1_b, sum1_in_a, sum1_in_b, sum2_a, sum2_b, sum2_in_a, sum2_in_b,
    block_a, block_b, all_a, all_b, feat_out, self_out,
    send_sem, recv_sem, load_sem, store_sem,
):
    rels, node_rows, width = gathered.shape
    slots = last.shape[3]
    half, lanes = width // 2, q * slots
    n = lax.axis_index("nodes")
    k = lax.axis_index("rel")
    z, y, core = n // q, n % q, k % 2
    low, high = slice(0, half), slice(half, width)

    def offset(t, count):
        near = (t + 1) // 2
        return (t % 2) * near + (1 - t % 2) * (count - near)

    def along(axis, j):
        return (j * q + y, k) if axis == "z" else ((z * q + j, k) if axis == "y" else (n, j))

    def place(axis):
        return (z, q) if axis == "z" else ((y, q) if axis == "y" else (k, groups))

    def copy(row, t, source, target, device):
        return pltpu.make_async_remote_copy(
            src_ref=source, dst_ref=target, send_sem=send_sem.at[row, t], recv_sem=recv_sem.at[row, t],
            device_id=device, device_id_type=MESH,
        )

    def start(*items, first=1, stop=None):
        def body(t, carry):
            for axis, row, source, target in items:
                me, count = place(axis)
                peer = (me + offset(t, count)) % count
                copy(row, t, source(peer), target(t), along(axis, peer)).start()
            return carry

        lax.fori_loop(first, stop or place(items[0][0])[1], body, 0)

    def finish(*items):
        def body(t, carry):
            for axis, row, source, landing in items:
                me, count = place(axis)
                peer = (me + count - offset(t, count)) % count
                copy(row, t, source(peer), landing(t, peer), along(axis, peer)).wait()
            return carry

        lax.fori_loop(1, place(items[0][0])[1], body, 0)

    barrier = pltpu.get_barrier_semaphore()
    for axis in ("z", "y", "rel"):
        me, count = place(axis)

        def greet(t, carry, axis=axis, me=me, count=count):
            pl.semaphore_signal(barrier, inc=1, device_id=along(axis, (me + t) % count), device_id_type=MESH)
            return carry

        lax.fori_loop(1, count, greet, 0)

    loads = [
        pltpu.make_async_copy(source, target, load_sem.at[i])
        for i, (source, target) in enumerate((
            (rows_hbm, rows), (counts_hbm, counts), (targets_hbm, targets), (grad_hbm, grad),
            (feat_hbm, feat), (self_hbm, self_w), (weight_hbm, weight),
        ))
    ]
    for load in loads:
        load.start()

    node = iota((node_rows, lanes), 0)
    eye = iota((lanes, lanes), 0) == iota((lanes, lanes), 1)
    blocks = q * q
    spread = (iota((slots, lanes), 0) == iota((slots, lanes), 1) % slots).astype(BF16)
    from_z = iota((blocks, lanes), 0) // q == iota((blocks, lanes), 1) // slots
    from_y = iota((blocks, lanes), 0) % q == iota((blocks, lanes), 1) // slots
    meta_a[...] = jnp.zeros_like(meta_a)
    meta_b[...] = jnp.zeros_like(meta_b)
    for load in loads[:3]:
        load.wait()
    for r in range(rels):
        live = iota((slots, blocks), 0) < counts[r]
        picks = dot(jnp.where(live, rows[r], -1).astype(F32).astype(BF16), spread, ((0,), (0,)))
        adds = dot(jnp.where(live, targets[r], -1).astype(F32).astype(BF16), spread, ((0,), (0,)))
        pick_a = jnp.sum(jnp.where(from_y, picks, 0.0).reshape(q, q, lanes), axis=1)
        pick_b = jnp.sum(jnp.where(from_z, picks, 0.0).reshape(q, q, lanes), axis=0)
        add_a = jnp.sum(jnp.where(from_y, adds, 0.0).reshape(q, q, lanes), axis=1)
        hits = jnp.zeros((node_rows, lanes), F32)
        for b in range(q):
            hits = hits + (pick_a[b : b + 1].astype(jnp.int32) == node).astype(F32)
        inverse = 1.0 / jnp.maximum(jnp.sum(hits, axis=1, keepdims=True), 1.0)
        for pick, meta in ((pick_a, meta_a), (pick_b, meta_b)):
            for b in range(q):
                row = pick[b : b + 1]
                meta[b, r : r + 1, :] = row
                meta[b, rels + r : rels + r + 1, :] = jnp.sum(
                    jnp.where(row.astype(jnp.int32) == node, inverse, 0.0), axis=0, keepdims=True
                )
        for b in range(q):
            meta_a[b, 2 * rels + r : 2 * rels + r + 1, :] = add_a[b : b + 1]
    loads[3].wait()

    pl.semaphore_wait(barrier, 2 * (q - 1) + groups - 1)
    own = pl.ds(pl.multiple_of(core * (node_rows // 2), node_rows // 2), node_rows // 2)
    ends = (("z", z, 0, low, raw_a), ("y", y, 1, high, raw_b))
    ring = range(1, min(3, q))

    def pass_on(axis, me, side, t, source, raw):
        step = 1 if t % 2 else q - 1
        return copy(RAW + side, t, source, raw.at[t, own], along(axis, (me + step) % q))

    def share_core(side, t, raw):
        return copy(CORE + side, t, raw.at[t, own], raw.at[t, own], (n, k + 1 - 2 * core))

    for t in ring:
        for axis, me, side, columns, raw in ends:
            pass_on(axis, me, side, t, grad.at[own, columns], raw).start()
    start(
        ("z", META, lambda j: meta_a.at[j], lambda t: meta_in_a.at[t]),
        ("y", META + 1, lambda j: meta_b.at[j], lambda t: meta_in_b.at[t]),
    )
    meta_in_a[0] = meta_a[z]
    meta_in_b[0] = meta_b[y]
    raw_a[0] = grad[:, low]
    raw_b[0] = grad[:, high]

    def forward(t):
        for axis, me, side, columns, raw in ends:
            pass_on(axis, me, side, t, grad.at[own, columns], raw).wait_recv()
            if t + 2 < q:
                pass_on(axis, me, side, t + 2, raw.at[t, own], raw).start()
            share_core(side, t, raw).start()

    def pick(t):
        other = pl.ds(pl.multiple_of((1 - core) * (node_rows // 2), node_rows // 2), node_rows // 2)
        for side, raw, meta, part in ((0, raw_a, meta_in_a, part_a), (1, raw_b, meta_in_b, part_b)):
            if t > 0:
                copy(CORE + side, t, raw.at[t, own], raw.at[t, other], (n, k)).wait_recv()
            for r in range(rels):
                hot = (meta[t, r : r + 1, :].astype(jnp.int32) == node).astype(BF16)
                factor = jnp.sum(jnp.where(eye, meta[t, rels + r : rels + r + 1, :], 0.0), axis=1, keepdims=True)
                message = (dot(hot, raw[t], ((0,), (0,))) * factor).astype(BF16)
                part[:, r, t] = message.reshape(q, slots, half)

    groups_of = [(0, 1)] + [(t, min(t + 2, q)) for t in range(1, q, 2)]

    def part_items(g):
        span = pl.ds(groups_of[g][0], groups_of[g][1] - groups_of[g][0])
        return (
            ("y", PART + 2 * g, lambda j: part_a.at[j, :, span], lambda t, j=0: last.at[:, t, span, :, low]),
            ("z", PART + 2 * g + 1, lambda j: part_b.at[j, :, span], lambda t, j=0: last.at[:, span, t, :, high]),
        )

    pick(0)
    start(*part_items(0))

    loads[4].wait()
    feat_t[...] = feat[...].T
    self_all[...] = dot(feat_t[...], grad[...], ((1,), (0,)))
    self_rows = width // groups
    strip = self_rows // q
    for b in range(q):
        mine = self_all[pl.ds(pl.multiple_of(k * self_rows + b * strip, strip), strip), :]
        self1[b] = jnp.concatenate([mine[:, low], mine[:, high]], axis=0).astype(BF16)
    self1_in[0] = self1[y]
    loads[5].wait()
    own_rows = node_rows // groups
    mine = pl.ds(pl.multiple_of(k * own_rows, own_rows), own_rows)
    self_term[...] = dot(grad[mine, :], self_w[...], ((1,), (1,)))

    for t in ring:
        forward(t)
    finish(
        ("z", META, lambda j: meta_a.at[j], lambda t, j: meta_in_a.at[t]),
        ("y", META + 1, lambda j: meta_b.at[j], lambda t, j: meta_in_b.at[t]),
    )
    wide = q * lanes
    same_slot = iota((lanes, wide), 0) == (iota((lanes, wide), 1) // lanes) * slots + iota((lanes, wide), 1) % slots
    same_from = iota((q, wide), 0) == (iota((q, wide), 1) // slots) % q
    tgt_send[...] = jnp.zeros_like(tgt_send)
    for r in range(rels):
        copies = dot(meta_in_a[:, 2 * rels + r, :].astype(BF16), same_slot.astype(BF16), ((1,), (0,)))
        row = jnp.sum(jnp.where(same_from, copies, 0.0), axis=0, keepdims=True)
        for b in range(q):
            tgt_send[b, r : r + 1, :] = row[:, b * lanes : (b + 1) * lanes]
    start(("y", TGT, lambda j: tgt_send.at[j], lambda t: tgt_last.at[t]))
    tgt_last[0] = tgt_send[y]
    start(("y", SELF1, lambda j: self1.at[j], lambda t: self1_in.at[t]))

    for g in range(1, len(groups_of)):
        for t in range(*groups_of[g]):
            if t not in ring:
                forward(t)
        for t in range(*groups_of[g]):
            pick(t)
        if g == max(1, len(groups_of) - 2):
            finish(("y", SELF1, lambda j: self1.at[j], lambda t, j: self1_in.at[t]))
            total = self1_in[0].astype(F32)
            for b in range(1, q):
                total = total + self1_in[b].astype(F32)
            self2[...] = total
            start(("z", SELF2, lambda j: self2, lambda t: self2_in.at[z]))
            self2_in[z] = total
        start(*part_items(g))
    for r in range(rels):
        last[r, 0, :, :, low] = part_a[y, r]
        last[r, :, 0, :, high] = part_b[z, r]

    finish(("y", TGT, lambda j: tgt_send.at[j], lambda t, j: tgt_last.at[t]))
    for r in range(rels):
        for b in range(q):
            one_hot[r, :, b * lanes : (b + 1) * lanes] = (
                tgt_last[b, r : r + 1, :].astype(jnp.int32) == node
            ).astype(BF16)

    finish(("z", SELF2, lambda j: self2, lambda t, j: self2_in.at[j]))
    total = self2_in[0]
    for b in range(1, q):
        total = total + self2_in[b]
    self3[...] = (total * scale).astype(BF16)
    start(("y", SELF3, lambda j: self3, lambda t: self3_in.at[y]))
    self3_in[y] = self3[...]

    for g in range(len(groups_of)):
        finish(*part_items(g))
    strip_rows = width // q
    for r in range(rels):
        gathered[r] = dot(one_hot[r], last[r].reshape(q * lanes, width), ((1,), (0,))).astype(BF16)
        grads = dot(feat_t[...], gathered[r], ((1,), (0,))).astype(BF16)
        sum1_a[r] = grads[:, low].reshape(q, strip_rows, half)
        sum1_b[r] = grads[:, high].reshape(q, strip_rows, half)
        start(
            ("y", SUM1 + 2 * r, lambda j: sum1_a.at[r, j], lambda t: sum1_in_a.at[r, t]),
            ("z", SUM1 + 2 * r + 1, lambda j: sum1_b.at[r, j], lambda t: sum1_in_b.at[r, t]),
        )
        sum1_in_a[r, 0] = sum1_a[r, y]
        sum1_in_b[r, 0] = sum1_b[r, z]

    loads[6].wait()
    total = dot(gathered[0], weight[0], ((1,), (1,)))
    for r in range(1, rels):
        total = total + dot(gathered[r], weight[r], ((1,), (1,)))
    share[...] = total.reshape(groups, own_rows, width)
    start(("rel", FEAT, lambda j: share.at[j], lambda t: share_in.at[t]))
    share_in[0] = share[k]

    small = strip_rows // q
    for r in range(rels):
        for axis, s, other, me, sums, sums_in, sends, sends_in in (
            ("y", 0, "z", z, sum1_a, sum1_in_a, sum2_a, sum2_in_a),
            ("z", 1, "y", y, sum1_b, sum1_in_b, sum2_b, sum2_in_b),
        ):
            finish((axis, SUM1 + 2 * r + s, lambda j: sums.at[r, j], lambda t, j: sums_in.at[r, t]))
            total = sums_in[r, 0].astype(F32)
            for b in range(1, q):
                total = total + sums_in[r, b].astype(F32)
            sends[r] = total.reshape(q, small, half)
            start((other, SUM2 + 2 * r + s, lambda j: sends.at[r, j], lambda t: sends_in.at[r, t]))
            sends_in[r, 0] = sends[r, me]
    for r in range(rels):
        for axis, s, me, sends, sends_in, block in (
            ("z", 0, z, sum2_a, sum2_in_a, block_a), ("y", 1, y, sum2_b, sum2_in_b, block_b),
        ):
            finish((axis, SUM2 + 2 * r + s, lambda j: sends.at[r, j], lambda t, j: sends_in.at[r, t]))
            total = sends_in[r, 0]
            for b in range(1, q):
                total = total + sends_in[r, b]
            total = total * scale
            block[r, me] = jnp.concatenate([total[:, : half // 2], total[:, half // 2 :]], axis=0).astype(BF16)
            start((axis, ALL1 + 2 * r + s, lambda j: block.at[r, me], lambda t: block.at[r, me]))

    stores = []

    def place_of(r, j):
        return pl.ds(pl.multiple_of(r * width + j * strip_rows, strip_rows), strip_rows)

    for r in range(rels):
        for axis, s, me, other, you, block, whole, side in (
            ("z", 0, z, "y", y, block_a, all_a, low), ("y", 1, y, "z", z, block_b, all_b, high),
        ):
            finish((axis, ALL1 + 2 * r + s, lambda j: block.at[r, me], lambda t, j: block.at[r, j]))
            pieces = block[r].astype(F32)
            sides = [pieces[:, i * small : (i + 1) * small, :].reshape(strip_rows, half // 2) for i in (0, 1)]
            whole[r] = jnp.concatenate(sides, axis=1).astype(BF16)
            start((other, ALL2 + 2 * r + s, lambda j: whole.at[r], lambda t: out_rel.at[place_of(r, you), side]))
            stores.append(pltpu.make_async_copy(
                whole.at[r], out_rel.at[place_of(r, you), side], store_sem.at[2 + 2 * r + s]
            ))
            stores[-1].start()

    finish(("rel", FEAT, lambda j: share.at[j], lambda t, j: share_in.at[t]))
    total = self_term[...]
    for b in range(groups):
        total = total + share_in[b]
    feat_out[...] = total.astype(BF16)
    stores.append(pltpu.make_async_copy(feat_out, out_feat, store_sem.at[0]))
    stores[-1].start()

    finish(("y", SELF3, lambda j: self3, lambda t, j: self3_in.at[j]))
    for b in range(0, q, 2):
        pair = [self3_in[b + i].astype(F32) for i in (0, 1)]
        wide_rows = [jnp.concatenate([p[:strip], p[strip:]], axis=1) for p in pair]
        self_out[b * strip : (b + 2) * strip, :] = jnp.concatenate(wide_rows, axis=0).astype(BF16)
    stores.append(pltpu.make_async_copy(self_out, out_self, store_sem.at[1]))
    stores[-1].start()

    for r in range(rels):
        finish(
            ("y", ALL2 + 2 * r, lambda j: all_a.at[r], lambda t, j: out_rel.at[place_of(r, j), low]),
            ("z", ALL2 + 2 * r + 1, lambda j: all_b.at[r], lambda t, j: out_rel.at[place_of(r, j), high]),
        )
    for store in stores:
        store.wait()
    for t in range(1, q):
        for axis, me, side, columns, raw in ends:
            pass_on(axis, me, side, t, grad.at[own, columns], raw).wait_send()
            share_core(side, t, raw).wait_send()


def solution(mesh):
    q = int(round(mesh.shape["nodes"] ** 0.5))
    groups = mesh.shape["rel"]

    def per_device(grad_out, node_feats, rel_weight, self_weight, send_rows, recv_rows, send_counts):
        node_rows, width = grad_out.shape
        rels = rel_weight.shape[0]
        slots = send_rows.shape[3]
        half, lanes = width // 2, q * slots
        strip_rows = width // q
        small = strip_rows // q
        strip = width // groups // q
        own_rows = node_rows // groups
        blocks = q * q
        in_hbm = pl.BlockSpec(memory_space=pltpu.HBM)
        flops = 2 * width * (3 * rels * node_rows * q * lanes + 3 * rels * node_rows * width)

        def two(shape, dtype):
            return [pltpu.VMEM(shape, dtype)] * 2

        outs = pl.pallas_call(
            functools.partial(kernel, q, groups, (node_rows * q * q) ** (-0.5)),
            out_shape=(
                jax.ShapeDtypeStruct((own_rows, width), BF16),
                jax.ShapeDtypeStruct((rels * width, width), BF16),
                jax.ShapeDtypeStruct((width // groups, width), BF16),
            ),
            in_specs=[in_hbm] * 7,
            out_specs=(in_hbm,) * 3,
            scratch_shapes=[
                pltpu.VMEM((node_rows, width), BF16),
                pltpu.VMEM((node_rows, width), BF16),
                pltpu.VMEM((rels, width, width), BF16),
                pltpu.VMEM((width, width), BF16),
                pltpu.VMEM((rels, slots, blocks), jnp.int32),
                pltpu.VMEM((rels, slots, blocks), jnp.int32),
                pltpu.VMEM((rels, 1, blocks), jnp.int32),
            ]
            + two((q, 8, lanes), F32)
            + two((q, 8, lanes), F32)
            + two((q, node_rows, half), BF16)
            + two((q, rels, q, slots, half), BF16)
            + [pltpu.VMEM((rels, q, q, slots, width), BF16)]
            + two((q, 8, lanes), F32)
            + [
                pltpu.VMEM((rels, node_rows, q * lanes), BF16),
                pltpu.VMEM((width, node_rows), BF16),
                pltpu.VMEM((rels, node_rows, width), BF16),
                pltpu.VMEM((width, width), F32),
                pltpu.VMEM((q, 2 * strip, half), BF16),
                pltpu.VMEM((q, 2 * strip, half), BF16),
                pltpu.VMEM((2 * strip, half), F32),
                pltpu.VMEM((q, 2 * strip, half), F32),
                pltpu.VMEM((2 * strip, half), BF16),
                pltpu.VMEM((q, 2 * strip, half), BF16),
                pltpu.VMEM((own_rows, width), F32),
            ]
            + two((groups, own_rows, width), F32)
            + two((rels, q, strip_rows, half), BF16)
            + two((rels, q, strip_rows, half), BF16)
            + two((rels, q, small, half), F32)
            + two((rels, q, small, half), F32)
            + two((rels, q, 2 * small, half // 2), BF16)
            + two((rels, strip_rows, half), BF16)
            + [
                pltpu.VMEM((own_rows, width), BF16),
                pltpu.VMEM((width // groups, width), BF16),
                pltpu.SemaphoreType.DMA((EXCHANGES, max(q, groups))),
                pltpu.SemaphoreType.DMA((EXCHANGES, max(q, groups))),
                pltpu.SemaphoreType.DMA((7,)),
                pltpu.SemaphoreType.DMA((2 + 2 * rels,)),
            ],
            compiler_params=pltpu.CompilerParams(
                collective_id=0, has_side_effects=True, vmem_limit_bytes=60 * 1024 * 1024
            ),
            cost_estimate=pl.CostEstimate(flops=flops, bytes_accessed=4 * 1024 * 1024, transcendentals=0),
        )(
            grad_out, node_feats, rel_weight, self_weight,
            send_rows.transpose(0, 1, 3, 2).reshape(rels, slots, blocks),
            recv_rows.transpose(0, 1, 3, 2).reshape(rels, slots, blocks),
            send_counts,
        )
        return outs[0], outs[1].reshape(rels, width, width), outs[2]

    return jax.shard_map(
        per_device,
        mesh=mesh,
        in_specs=(
            P("nodes", None),
            P("nodes", None),
            P("rel", None, None),
            P(),
            P("rel", "nodes", None, None),
            P("rel", "nodes", None, None),
            P("rel", "nodes", None),
        ),
        out_specs=(P(("nodes", "rel"), None), P("rel", None, None), P("rel", None)),
        check_vma=False,
    )
```

```python
import functools

import jax
import jax.numpy as jnp
from jax import lax
from jax.experimental import pallas as pl
from jax.experimental.pallas import tpu as pltpu
from jax.sharding import PartitionSpec as P

MESH = pl.DeviceIdType.MESH
F32 = jnp.float32
BF16 = jnp.bfloat16

META, RAW, CORE, PART, SUM1, SUM2, ALL1, ALL2, TGT, SELF1, SELF2, SELF3, FEAT = 0, 2, 4, 6, 18, 22, 26, 30, 34, 35, 36, 37, 38
EXCHANGES = 39


def iota(shape, dim):
    return lax.broadcasted_iota(jnp.int32, shape, dim)


def dot(a, b, contract):
    return lax.dot_general(a, b, ((contract[0], contract[1]), ((), ())), preferred_element_type=F32)


def kernel(
    q, groups, scale,
    grad_hbm, feat_hbm, weight_hbm, self_hbm, rows_hbm, targets_hbm, counts_hbm,
    out_feat, out_rel, out_self,
    grad, feat, weight, self_w, rows, targets, counts,
    meta_a, meta_b, meta_in_a, meta_in_b, raw_a, raw_b, part_a, part_b, last,
    tgt_send, tgt_last, one_hot, feat_t, gathered, self_all, self1, self1_in, self2, self2_in, self3, self3_in,
    self_term, share, share_in, sum1_a, sum1_b, sum1_in_a, sum1_in_b, sum2_a, sum2_b, sum2_in_a, sum2_in_b,
    block_a, block_b, all_a, all_b, feat_out, self_out,
    send_sem, recv_sem, load_sem, store_sem,
):
    rels, node_rows, width = gathered.shape
    slots = last.shape[3]
    half, lanes = width // 2, q * slots
    n = lax.axis_index("nodes")
    k = lax.axis_index("rel")
    z, y, core = n // q, n % q, k % 2
    low, high = slice(0, half), slice(half, width)

    def offset(t, count):
        near = (t + 1) // 2
        return (t % 2) * near + (1 - t % 2) * (count - near)

    def along(axis, j):
        return (j * q + y, k) if axis == "z" else ((z * q + j, k) if axis == "y" else (n, j))

    def place(axis):
        return (z, q) if axis == "z" else ((y, q) if axis == "y" else (k, groups))

    def copy(row, t, source, target, device):
        return pltpu.make_async_remote_copy(
            src_ref=source, dst_ref=target, send_sem=send_sem.at[row, t], recv_sem=recv_sem.at[row, t],
            device_id=device, device_id_type=MESH,
        )

    def start(*items, first=1, stop=None):
        def body(t, carry):
            for axis, row, source, target in items:
                me, count = place(axis)
                peer = (me + offset(t, count)) % count
                copy(row, t, source(peer), target(t), along(axis, peer)).start()
            return carry

        lax.fori_loop(first, stop or place(items[0][0])[1], body, 0)

    def finish(*items):
        def body(t, carry):
            for axis, row, source, landing in items:
                me, count = place(axis)
                peer = (me + count - offset(t, count)) % count
                copy(row, t, source(peer), landing(t, peer), along(axis, peer)).wait()
            return carry

        lax.fori_loop(1, place(items[0][0])[1], body, 0)

    barrier = pltpu.get_barrier_semaphore()
    for axis in ("z", "y", "rel"):
        me, count = place(axis)

        def greet(t, carry, axis=axis, me=me, count=count):
            pl.semaphore_signal(barrier, inc=1, device_id=along(axis, (me + t) % count), device_id_type=MESH)
            return carry

        lax.fori_loop(1, count, greet, 0)

    loads = [
        pltpu.make_async_copy(source, target, load_sem.at[i])
        for i, (source, target) in enumerate((
            (rows_hbm, rows), (counts_hbm, counts), (targets_hbm, targets), (grad_hbm, grad),
            (feat_hbm, feat), (self_hbm, self_w), (weight_hbm, weight),
        ))
    ]
    for load in loads:
        load.start()

    pl.semaphore_wait(barrier, 2 * (q - 1) + groups - 1)
    own = pl.ds(pl.multiple_of(core * (node_rows // 2), node_rows // 2), node_rows // 2)
    ends = (("z", z, 0, low, raw_a), ("y", y, 1, high, raw_b))
    ring = range(1, min(3, q))

    def pass_on(axis, me, side, t, source, raw):
        step = 1 if t % 2 else q - 1
        return copy(RAW + side, t, source, raw.at[t, own], along(axis, (me + step) % q))

    def share_core(side, t, raw):
        return copy(CORE + side, t, raw.at[t, own], raw.at[t, own], (n, k + 1 - 2 * core))

    for t in ring:
        for axis, me, side, columns, raw in ends:
            pass_on(axis, me, side, t, grad_hbm.at[own, columns], raw).start()

    node = iota((node_rows, lanes), 0)
    eye = iota((lanes, lanes), 0) == iota((lanes, lanes), 1)
    blocks = q * q
    spread = (iota((slots, lanes), 0) == iota((slots, lanes), 1) % slots).astype(BF16)
    from_z = iota((blocks, lanes), 0) // q == iota((blocks, lanes), 1) // slots
    from_y = iota((blocks, lanes), 0) % q == iota((blocks, lanes), 1) // slots
    meta_a[...] = jnp.zeros_like(meta_a)
    meta_b[...] = jnp.zeros_like(meta_b)
    for load in loads[:3]:
        load.wait()
    for r in range(rels):
        live = iota((slots, blocks), 0) < counts[r]
        picks = dot(jnp.where(live, rows[r], -1).astype(F32).astype(BF16), spread, ((0,), (0,)))
        adds = dot(jnp.where(live, targets[r], -1).astype(F32).astype(BF16), spread, ((0,), (0,)))
        pick_a = jnp.sum(jnp.where(from_y, picks, 0.0).reshape(q, q, lanes), axis=1)
        pick_b = jnp.sum(jnp.where(from_z, picks, 0.0).reshape(q, q, lanes), axis=0)
        add_a = jnp.sum(jnp.where(from_y, adds, 0.0).reshape(q, q, lanes), axis=1)
        hits = jnp.zeros((node_rows, lanes), F32)
        for b in range(q):
            hits = hits + (pick_a[b : b + 1].astype(jnp.int32) == node).astype(F32)
        inverse = 1.0 / jnp.maximum(jnp.sum(hits, axis=1, keepdims=True), 1.0)
        for pick, meta in ((pick_a, meta_a), (pick_b, meta_b)):
            for b in range(q):
                row = pick[b : b + 1]
                meta[b, r : r + 1, :] = row
                meta[b, rels + r : rels + r + 1, :] = jnp.sum(
                    jnp.where(row.astype(jnp.int32) == node, inverse, 0.0), axis=0, keepdims=True
                )
        for b in range(q):
            meta_a[b, 2 * rels + r : 2 * rels + r + 1, :] = add_a[b : b + 1]

    start(
        ("z", META, lambda j: meta_a.at[j], lambda t: meta_in_a.at[t]),
        ("y", META + 1, lambda j: meta_b.at[j], lambda t: meta_in_b.at[t]),
    )
    loads[3].wait()
    meta_in_a[0] = meta_a[z]
    meta_in_b[0] = meta_b[y]
    raw_a[0] = grad[:, low]
    raw_b[0] = grad[:, high]

    def forward(t):
        for axis, me, side, columns, raw in ends:
            pass_on(axis, me, side, t, grad_hbm.at[own, columns], raw).wait_recv()
            if t + 2 < q:
                pass_on(axis, me, side, t + 2, raw.at[t, own], raw).start()
            share_core(side, t, raw).start()

    def pick(t):
        other = pl.ds(pl.multiple_of((1 - core) * (node_rows // 2), node_rows // 2), node_rows // 2)
        for side, raw, meta, part in ((0, raw_a, meta_in_a, part_a), (1, raw_b, meta_in_b, part_b)):
            if t > 0:
                copy(CORE + side, t, raw.at[t, own], raw.at[t, other], (n, k)).wait_recv()
            for r in range(rels):
                hot = (meta[t, r : r + 1, :].astype(jnp.int32) == node).astype(BF16)
                factor = jnp.sum(jnp.where(eye, meta[t, rels + r : rels + r + 1, :], 0.0), axis=1, keepdims=True)
                message = (dot(hot, raw[t], ((0,), (0,))) * factor).astype(BF16)
                part[:, r, t] = message.reshape(q, slots, half)

    groups_of = [(0, 1)] + [(t, min(t + 2, q)) for t in range(1, q, 2)]

    def part_items(g, r=None):
        span = pl.ds(groups_of[g][0], groups_of[g][1] - groups_of[g][0])
        which = slice(None) if r is None else r
        row = PART + 2 * g + 2 * (r or 0)
        return (
            ("y", row, lambda j: part_a.at[j, which, span], lambda t, j=0: last.at[which, t, span, :, low]),
            ("z", row + 1, lambda j: part_b.at[j, which, span], lambda t, j=0: last.at[which, span, t, :, high]),
        )

    pick(0)
    start(*part_items(0))

    for t in ring:
        forward(t)
    finish(
        ("z", META, lambda j: meta_a.at[j], lambda t, j: meta_in_a.at[t]),
        ("y", META + 1, lambda j: meta_b.at[j], lambda t, j: meta_in_b.at[t]),
    )
    wide = q * lanes
    same_slot = iota((lanes, wide), 0) == (iota((lanes, wide), 1) // lanes) * slots + iota((lanes, wide), 1) % slots
    same_from = iota((q, wide), 0) == (iota((q, wide), 1) // slots) % q
    tgt_send[...] = jnp.zeros_like(tgt_send)
    for r in range(rels):
        copies = dot(meta_in_a[:, 2 * rels + r, :].astype(BF16), same_slot.astype(BF16), ((1,), (0,)))
        row = jnp.sum(jnp.where(same_from, copies, 0.0), axis=0, keepdims=True)
        for b in range(q):
            tgt_send[b, r : r + 1, :] = row[:, b * lanes : (b + 1) * lanes]
    start(("y", TGT, lambda j: tgt_send.at[j], lambda t: tgt_last.at[t]))
    tgt_last[0] = tgt_send[y]

    for g in range(1, len(groups_of)):
        for t in range(*groups_of[g]):
            if t not in ring:
                forward(t)
        for t in range(*groups_of[g]):
            pick(t)
        if g < len(groups_of) - 1:
            start(*part_items(g))
    for r in range(rels):
        start(*part_items(len(groups_of) - 1, r))
    for r in range(rels):
        last[r, 0, :, :, low] = part_a[y, r]
        last[r, :, 0, :, high] = part_b[z, r]

    loads[4].wait()
    feat_t[...] = feat[...].T
    self_all[...] = dot(feat_t[...], grad[...], ((1,), (0,)))
    self_rows = width // groups
    strip = self_rows // q
    for b in range(q):
        mine = self_all[pl.ds(pl.multiple_of(k * self_rows + b * strip, strip), strip), :]
        self1[b] = jnp.concatenate([mine[:, low], mine[:, high]], axis=0).astype(BF16)
    self1_in[0] = self1[y]
    loads[5].wait()
    own_rows = node_rows // groups
    mine = pl.ds(pl.multiple_of(k * own_rows, own_rows), own_rows)
    self_term[...] = dot(grad[mine, :], self_w[...], ((1,), (1,)))

    finish(("y", TGT, lambda j: tgt_send.at[j], lambda t, j: tgt_last.at[t]))
    for r in range(rels):
        for b in range(q):
            one_hot[r, :, b * lanes : (b + 1) * lanes] = (
                tgt_last[b, r : r + 1, :].astype(jnp.int32) == node
            ).astype(BF16)

    for g in range(len(groups_of) - 1):
        finish(*part_items(g))
    strip_rows = width // q
    for r in range(rels):
        finish(*part_items(len(groups_of) - 1, r))
        gathered[r] = dot(one_hot[r], last[r].reshape(q * lanes, width), ((1,), (0,))).astype(BF16)
        grads = dot(feat_t[...], gathered[r], ((1,), (0,))).astype(BF16)
        sum1_a[r] = grads[:, low].reshape(q, strip_rows, half)
        sum1_b[r] = grads[:, high].reshape(q, strip_rows, half)
        start(
            ("y", SUM1 + 2 * r, lambda j: sum1_a.at[r, j], lambda t: sum1_in_a.at[r, t]),
            ("z", SUM1 + 2 * r + 1, lambda j: sum1_b.at[r, j], lambda t: sum1_in_b.at[r, t]),
        )
        sum1_in_a[r, 0] = sum1_a[r, y]
        sum1_in_b[r, 0] = sum1_b[r, z]

    loads[6].wait()
    total = dot(gathered[0], weight[0], ((1,), (1,)))
    for r in range(1, rels):
        total = total + dot(gathered[r], weight[r], ((1,), (1,)))
    share[...] = total.reshape(groups, own_rows, width)
    start(("rel", FEAT, lambda j: share.at[j], lambda t: share_in.at[t]))
    share_in[0] = share[k]

    small = strip_rows // q

    def add_first(r):
        for axis, s, other, me, sums, sums_in, sends, sends_in in (
            ("y", 0, "z", z, sum1_a, sum1_in_a, sum2_a, sum2_in_a),
            ("z", 1, "y", y, sum1_b, sum1_in_b, sum2_b, sum2_in_b),
        ):
            finish((axis, SUM1 + 2 * r + s, lambda j: sums.at[r, j], lambda t, j: sums_in.at[r, t]))
            total = sums_in[r, 0].astype(F32)
            for b in range(1, q):
                total = total + sums_in[r, b].astype(F32)
            sends[r] = total.reshape(q, small, half)
            start((other, SUM2 + 2 * r + s, lambda j: sends.at[r, j], lambda t: sends_in.at[r, t]))
            sends_in[r, 0] = sends[r, me]

    def add_second(r):
        for axis, s, me, sends, sends_in, block in (
            ("z", 0, z, sum2_a, sum2_in_a, block_a), ("y", 1, y, sum2_b, sum2_in_b, block_b),
        ):
            finish((axis, SUM2 + 2 * r + s, lambda j: sends.at[r, j], lambda t, j: sends_in.at[r, t]))
            total = sends_in[r, 0]
            for b in range(1, q):
                total = total + sends_in[r, b]
            total = total * scale
            block[r, me] = jnp.concatenate([total[:, : half // 2], total[:, half // 2 :]], axis=0).astype(BF16)
            start((axis, ALL1 + 2 * r + s, lambda j: block.at[r, me], lambda t: block.at[r, me]))

    stores = []

    def place_of(r, j):
        return pl.ds(pl.multiple_of(r * width + j * strip_rows, strip_rows), strip_rows)

    def gather_last(r):
        for axis, s, me, other, you, block, whole, side in (
            ("z", 0, z, "y", y, block_a, all_a, low), ("y", 1, y, "z", z, block_b, all_b, high),
        ):
            finish((axis, ALL1 + 2 * r + s, lambda j: block.at[r, me], lambda t, j: block.at[r, j]))
            pieces = block[r].astype(F32)
            sides = [pieces[:, i * small : (i + 1) * small, :].reshape(strip_rows, half // 2) for i in (0, 1)]
            whole[r] = jnp.concatenate(sides, axis=1).astype(BF16)
            start((other, ALL2 + 2 * r + s, lambda j: whole.at[r], lambda t: out_rel.at[place_of(r, you), side]))
            stores.append(pltpu.make_async_copy(
                whole.at[r], out_rel.at[place_of(r, you), side], store_sem.at[2 + 2 * r + s]
            ))
            stores[-1].start()

    add_first(0)
    start(("y", SELF1, lambda j: self1.at[j], lambda t: self1_in.at[t]))
    for r in range(1, rels):
        add_first(r)
    add_second(0)
    finish(("y", SELF1, lambda j: self1.at[j], lambda t, j: self1_in.at[t]))
    total = self1_in[0].astype(F32)
    for b in range(1, q):
        total = total + self1_in[b].astype(F32)
    self2[...] = total
    start(("z", SELF2, lambda j: self2, lambda t: self2_in.at[z]))
    self2_in[z] = total
    for r in range(1, rels):
        add_second(r)
    gather_last(0)
    finish(("z", SELF2, lambda j: self2, lambda t, j: self2_in.at[j]))
    total = self2_in[0]
    for b in range(1, q):
        total = total + self2_in[b]
    self3[...] = (total * scale).astype(BF16)
    start(("y", SELF3, lambda j: self3, lambda t: self3_in.at[y]))
    self3_in[y] = self3[...]
    for r in range(1, rels):
        gather_last(r)

    finish(("rel", FEAT, lambda j: share.at[j], lambda t, j: share_in.at[t]))
    total = self_term[...]
    for b in range(groups):
        total = total + share_in[b]
    feat_out[...] = total.astype(BF16)
    stores.append(pltpu.make_async_copy(feat_out, out_feat, store_sem.at[0]))
    stores[-1].start()

    finish(("y", SELF3, lambda j: self3, lambda t, j: self3_in.at[j]))
    for b in range(0, q, 2):
        pair = [self3_in[b + i].astype(F32) for i in (0, 1)]
        wide_rows = [jnp.concatenate([p[:strip], p[strip:]], axis=1) for p in pair]
        self_out[b * strip : (b + 2) * strip, :] = jnp.concatenate(wide_rows, axis=0).astype(BF16)
    stores.append(pltpu.make_async_copy(self_out, out_self, store_sem.at[1]))
    stores[-1].start()

    for r in range(rels):
        finish(
            ("y", ALL2 + 2 * r, lambda j: all_a.at[r], lambda t, j: out_rel.at[place_of(r, j), low]),
            ("z", ALL2 + 2 * r + 1, lambda j: all_b.at[r], lambda t, j: out_rel.at[place_of(r, j), high]),
        )
    for store in stores:
        store.wait()
    for t in range(1, q):
        for axis, me, side, columns, raw in ends:
            pass_on(axis, me, side, t, grad_hbm.at[own, columns], raw).wait_send()
            share_core(side, t, raw).wait_send()


def solution(mesh):
    q = int(round(mesh.shape["nodes"] ** 0.5))
    groups = mesh.shape["rel"]

    def per_device(grad_out, node_feats, rel_weight, self_weight, send_rows, recv_rows, send_counts):
        node_rows, width = grad_out.shape
        rels = rel_weight.shape[0]
        slots = send_rows.shape[3]
        half, lanes = width // 2, q * slots
        strip_rows = width // q
        small = strip_rows // q
        strip = width // groups // q
        own_rows = node_rows // groups
        blocks = q * q
        in_hbm = pl.BlockSpec(memory_space=pltpu.HBM)
        flops = 2 * width * (3 * rels * node_rows * q * lanes + 3 * rels * node_rows * width)

        def two(shape, dtype):
            return [pltpu.VMEM(shape, dtype)] * 2

        outs = pl.pallas_call(
            functools.partial(kernel, q, groups, (node_rows * q * q) ** (-0.5)),
            out_shape=(
                jax.ShapeDtypeStruct((own_rows, width), BF16),
                jax.ShapeDtypeStruct((rels * width, width), BF16),
                jax.ShapeDtypeStruct((width // groups, width), BF16),
            ),
            in_specs=[in_hbm] * 7,
            out_specs=(in_hbm,) * 3,
            scratch_shapes=[
                pltpu.VMEM((node_rows, width), BF16),
                pltpu.VMEM((node_rows, width), BF16),
                pltpu.VMEM((rels, width, width), BF16),
                pltpu.VMEM((width, width), BF16),
                pltpu.VMEM((rels, slots, blocks), jnp.int32),
                pltpu.VMEM((rels, slots, blocks), jnp.int32),
                pltpu.VMEM((rels, 1, blocks), jnp.int32),
            ]
            + two((q, 8, lanes), F32)
            + two((q, 8, lanes), F32)
            + two((q, node_rows, half), BF16)
            + two((q, rels, q, slots, half), BF16)
            + [pltpu.VMEM((rels, q, q, slots, width), BF16)]
            + two((q, 8, lanes), F32)
            + [
                pltpu.VMEM((rels, node_rows, q * lanes), BF16),
                pltpu.VMEM((width, node_rows), BF16),
                pltpu.VMEM((rels, node_rows, width), BF16),
                pltpu.VMEM((width, width), F32),
                pltpu.VMEM((q, 2 * strip, half), BF16),
                pltpu.VMEM((q, 2 * strip, half), BF16),
                pltpu.VMEM((2 * strip, half), F32),
                pltpu.VMEM((q, 2 * strip, half), F32),
                pltpu.VMEM((2 * strip, half), BF16),
                pltpu.VMEM((q, 2 * strip, half), BF16),
                pltpu.VMEM((own_rows, width), F32),
            ]
            + two((groups, own_rows, width), F32)
            + two((rels, q, strip_rows, half), BF16)
            + two((rels, q, strip_rows, half), BF16)
            + two((rels, q, small, half), F32)
            + two((rels, q, small, half), F32)
            + two((rels, q, 2 * small, half // 2), BF16)
            + two((rels, strip_rows, half), BF16)
            + [
                pltpu.VMEM((own_rows, width), BF16),
                pltpu.VMEM((width // groups, width), BF16),
                pltpu.SemaphoreType.DMA((EXCHANGES, max(q, groups))),
                pltpu.SemaphoreType.DMA((EXCHANGES, max(q, groups))),
                pltpu.SemaphoreType.DMA((7,)),
                pltpu.SemaphoreType.DMA((2 + 2 * rels,)),
            ],
            compiler_params=pltpu.CompilerParams(
                collective_id=0, has_side_effects=True, vmem_limit_bytes=60 * 1024 * 1024
            ),
            cost_estimate=pl.CostEstimate(flops=flops, bytes_accessed=4 * 1024 * 1024, transcendentals=0),
        )(
            grad_out, node_feats, rel_weight, self_weight,
            send_rows.transpose(0, 1, 3, 2).reshape(rels, slots, blocks),
            recv_rows.transpose(0, 1, 3, 2).reshape(rels, slots, blocks),
            send_counts,
        )
        return outs[0], outs[1].reshape(rels, width, width), outs[2]

    return jax.shard_map(
        per_device,
        mesh=mesh,
        in_specs=(
            P("nodes", None),
            P("nodes", None),
            P("rel", None, None),
            P(),
            P("rel", "nodes", None, None),
            P("rel", "nodes", None, None),
            P("rel", "nodes", None),
        ),
        out_specs=(P(("nodes", "rel"), None), P("rel", None, None), P("rel", None)),
        check_vma=False,
    )
```

```python
import functools

import jax
import jax.numpy as jnp
from jax import lax
from jax.experimental import pallas as pl
from jax.experimental.pallas import tpu as pltpu
from jax.sharding import PartitionSpec as P

MESH = pl.DeviceIdType.MESH
F32 = jnp.float32
BF16 = jnp.bfloat16

META, RAW, CORE, PART, SUM1, SUM2, ALL1, ALL2, TGT, SELF1, SELF2, SELF3, FEAT = 0, 2, 4, 6, 18, 22, 26, 30, 34, 35, 36, 37, 38
EXCHANGES = 39


def iota(shape, dim):
    return lax.broadcasted_iota(jnp.int32, shape, dim)


def dot(a, b, contract):
    return lax.dot_general(a, b, ((contract[0], contract[1]), ((), ())), preferred_element_type=F32)


def kernel(
    q, groups, scale,
    grad_hbm, feat_hbm, weight_hbm, self_hbm, rows_hbm, targets_hbm, counts_hbm,
    out_feat, out_rel, out_self,
    grad, feat, weight, self_w, rows, targets, counts,
    meta_a, meta_b, meta_in_a, meta_in_b, raw_a, raw_b, part_a, part_b, last,
    tgt_send, tgt_last, one_hot, feat_t, gathered, self_all, self1, self1_in, self2, self2_in, self3, self3_in,
    self_term, share, share_in, sum1_a, sum1_b, sum1_in_a, sum1_in_b, sum2_a, sum2_b, sum2_in_a, sum2_in_b,
    block_a, block_b, all_a, all_b, feat_out, self_out,
    send_sem, recv_sem, load_sem, store_sem,
):
    rels, node_rows, width = gathered.shape
    slots = last.shape[3]
    half, lanes = width // 2, q * slots
    n = lax.axis_index("nodes")
    k = lax.axis_index("rel")
    z, y, core = n // q, n % q, k % 2
    low, high = slice(0, half), slice(half, width)

    def offset(t, count):
        near = (t + 1) // 2
        return (t % 2) * near + (1 - t % 2) * (count - near)

    def along(axis, j):
        return (j * q + y, k) if axis == "z" else ((z * q + j, k) if axis == "y" else (n, j))

    def place(axis):
        return (z, q) if axis == "z" else ((y, q) if axis == "y" else (k, groups))

    def copy(row, t, source, target, device):
        return pltpu.make_async_remote_copy(
            src_ref=source, dst_ref=target, send_sem=send_sem.at[row, t], recv_sem=recv_sem.at[row, t],
            device_id=device, device_id_type=MESH,
        )

    def start(*items, first=1, stop=None):
        def body(t, carry):
            for axis, row, source, target in items:
                me, count = place(axis)
                peer = (me + offset(t, count)) % count
                copy(row, t, source(peer), target(t), along(axis, peer)).start()
            return carry

        lax.fori_loop(first, stop or place(items[0][0])[1], body, 0)

    def finish(*items, first=1):
        def body(t, carry):
            for axis, row, source, landing in items:
                me, count = place(axis)
                peer = (me + count - offset(t, count)) % count
                copy(row, t, source(peer), landing(t, peer), along(axis, peer)).wait()
            return carry

        lax.fori_loop(first, place(items[0][0])[1], body, 0)

    barrier = pltpu.get_barrier_semaphore()
    for axis in ("z", "y", "rel"):
        me, count = place(axis)

        def greet(t, carry, axis=axis, me=me, count=count):
            pl.semaphore_signal(barrier, inc=1, device_id=along(axis, (me + t) % count), device_id_type=MESH)
            return carry

        lax.fori_loop(1, count, greet, 0)

    loads = [
        pltpu.make_async_copy(source, target, load_sem.at[i])
        for i, (source, target) in enumerate((
            (rows_hbm, rows), (counts_hbm, counts), (targets_hbm, targets), (grad_hbm, grad),
            (feat_hbm, feat), (self_hbm, self_w), (weight_hbm, weight),
        ))
    ]
    for load in loads:
        load.start()

    pl.semaphore_wait(barrier, 2 * (q - 1) + groups - 1)
    own = pl.ds(pl.multiple_of(core * (node_rows // 2), node_rows // 2), node_rows // 2)
    ends = (("z", z, 0, low, raw_a), ("y", y, 1, high, raw_b))
    direct = range(1, min(5, q))

    def pass_on(axis, me, side, t, source, raw):
        step = offset(t, q) if t in direct else (1 if t % 2 else q - 1)
        return copy(RAW + side, t, source, raw.at[t, own], along(axis, (me + step) % q))

    def share_core(side, t, raw):
        return copy(CORE + side, t, raw.at[t, own], raw.at[t, own], (n, k + 1 - 2 * core))

    for t in direct:
        for axis, me, side, columns, raw in ends:
            pass_on(axis, me, side, t, grad_hbm.at[own, columns], raw).start()

    node = iota((node_rows, lanes), 0)
    eye = iota((lanes, lanes), 0) == iota((lanes, lanes), 1)
    blocks = q * q
    spread = (iota((slots, lanes), 0) == iota((slots, lanes), 1) % slots).astype(BF16)
    from_z = iota((blocks, lanes), 0) // q == iota((blocks, lanes), 1) // slots
    from_y = iota((blocks, lanes), 0) % q == iota((blocks, lanes), 1) // slots
    meta_a[...] = jnp.zeros_like(meta_a)
    meta_b[...] = jnp.zeros_like(meta_b)
    for load in loads[:3]:
        load.wait()
    for r in range(rels):
        live = iota((slots, blocks), 0) < counts[r]
        picks = dot(jnp.where(live, rows[r], -1).astype(F32).astype(BF16), spread, ((0,), (0,)))
        adds = dot(jnp.where(live, targets[r], -1).astype(F32).astype(BF16), spread, ((0,), (0,)))
        pick_a = jnp.sum(jnp.where(from_y, picks, 0.0).reshape(q, q, lanes), axis=1)
        pick_b = jnp.sum(jnp.where(from_z, picks, 0.0).reshape(q, q, lanes), axis=0)
        add_a = jnp.sum(jnp.where(from_y, adds, 0.0).reshape(q, q, lanes), axis=1)
        hits = jnp.zeros((node_rows, lanes), F32)
        for b in range(q):
            hits = hits + (pick_a[b : b + 1].astype(jnp.int32) == node).astype(F32)
        inverse = 1.0 / jnp.maximum(jnp.sum(hits, axis=1, keepdims=True), 1.0)
        for pick, meta in ((pick_a, meta_a), (pick_b, meta_b)):
            for b in range(q):
                row = pick[b : b + 1]
                meta[b, r : r + 1, :] = row
                meta[b, rels + r : rels + r + 1, :] = jnp.sum(
                    jnp.where(row.astype(jnp.int32) == node, inverse, 0.0), axis=0, keepdims=True
                )
        for b in range(q):
            meta_a[b, 2 * rels + r : 2 * rels + r + 1, :] = add_a[b : b + 1]

    start(
        ("z", META, lambda j: meta_a.at[j], lambda t: meta_in_a.at[t]),
        ("y", META + 1, lambda j: meta_b.at[j], lambda t: meta_in_b.at[t]),
    )
    loads[3].wait()
    meta_in_a[0] = meta_a[z]
    meta_in_b[0] = meta_b[y]
    raw_a[0] = grad[:, low]
    raw_b[0] = grad[:, high]

    def forward(t):
        for axis, me, side, columns, raw in ends:
            pass_on(axis, me, side, t, grad_hbm.at[own, columns], raw).wait_recv()
            if t + 2 < q and t + 2 not in direct:
                pass_on(axis, me, side, t + 2, raw.at[t, own], raw).start()
            share_core(side, t, raw).start()

    def pick(t):
        other = pl.ds(pl.multiple_of((1 - core) * (node_rows // 2), node_rows // 2), node_rows // 2)
        for side, raw, sent, meta, part in (
            (0, raw_a, meta_a, meta_in_a, part_a), (1, raw_b, meta_b, meta_in_b, part_b),
        ):
            if t > 0:
                if t in direct:
                    copy(META + side, t, sent.at[0], meta.at[t], (n, k)).wait()
                copy(CORE + side, t, raw.at[t, own], raw.at[t, other], (n, k)).wait_recv()
            for r in range(rels):
                hot = (meta[t, r : r + 1, :].astype(jnp.int32) == node).astype(BF16)
                factor = jnp.sum(jnp.where(eye, meta[t, rels + r : rels + r + 1, :], 0.0), axis=1, keepdims=True)
                message = (dot(hot, raw[t], ((0,), (0,))) * factor).astype(BF16)
                part[:, r, t] = message.reshape(q, slots, half)

    groups_of = [(0, 1)] + [(t, min(t + 2, q)) for t in range(1, q, 2)]

    def part_items(g, r=None):
        span = pl.ds(groups_of[g][0], groups_of[g][1] - groups_of[g][0])
        which = slice(None) if r is None else r
        row = PART + 2 * g + 2 * (r or 0)
        return (
            ("y", row, lambda j: part_a.at[j, which, span], lambda t, j=0: last.at[which, t, span, :, low]),
            ("z", row + 1, lambda j: part_b.at[j, which, span], lambda t, j=0: last.at[which, span, t, :, high]),
        )

    pick(0)
    start(*part_items(0))

    def send_targets():
        if direct.stop < q:
            finish(
                ("z", META, lambda j: meta_a.at[j], lambda t, j: meta_in_a.at[t]),
                ("y", META + 1, lambda j: meta_b.at[j], lambda t, j: meta_in_b.at[t]),
                first=direct.stop,
            )
        wide = q * lanes
        same_slot = iota((lanes, wide), 0) == (iota((lanes, wide), 1) // lanes) * slots + iota((lanes, wide), 1) % slots
        same_from = iota((q, wide), 0) == (iota((q, wide), 1) // slots) % q
        tgt_send[...] = jnp.zeros_like(tgt_send)
        for r in range(rels):
            copies = dot(meta_in_a[:, 2 * rels + r, :].astype(BF16), same_slot.astype(BF16), ((1,), (0,)))
            row = jnp.sum(jnp.where(same_from, copies, 0.0), axis=0, keepdims=True)
            for b in range(q):
                tgt_send[b, r : r + 1, :] = row[:, b * lanes : (b + 1) * lanes]
        start(("y", TGT, lambda j: tgt_send.at[j], lambda t: tgt_last.at[t]))
        tgt_last[0] = tgt_send[y]

    for g in range(1, len(groups_of)):
        for t in range(*groups_of[g]):
            forward(t)
        for t in range(*groups_of[g]):
            pick(t)
        if g < len(groups_of) - 1:
            start(*part_items(g))
        if g == min(2, len(groups_of) - 1):
            send_targets()
    for r in range(rels):
        start(*part_items(len(groups_of) - 1, r))
    for r in range(rels):
        last[r, 0, :, :, low] = part_a[y, r]
        last[r, :, 0, :, high] = part_b[z, r]

    loads[4].wait()
    feat_t[...] = feat[...].T
    self_all[...] = dot(feat_t[...], grad[...], ((1,), (0,)))
    self_rows = width // groups
    strip = self_rows // q
    for b in range(q):
        mine = self_all[pl.ds(pl.multiple_of(k * self_rows + b * strip, strip), strip), :]
        self1[b] = jnp.concatenate([mine[:, low], mine[:, high]], axis=0).astype(BF16)
    self1_in[0] = self1[y]
    loads[5].wait()
    own_rows = node_rows // groups
    mine = pl.ds(pl.multiple_of(k * own_rows, own_rows), own_rows)
    self_term[...] = dot(grad[mine, :], self_w[...], ((1,), (1,)))

    finish(("y", TGT, lambda j: tgt_send.at[j], lambda t, j: tgt_last.at[t]))
    for r in range(rels):
        for b in range(q):
            one_hot[r, :, b * lanes : (b + 1) * lanes] = (
                tgt_last[b, r : r + 1, :].astype(jnp.int32) == node
            ).astype(BF16)

    for g in range(len(groups_of) - 1):
        finish(*part_items(g))
    strip_rows = width // q
    for r in range(rels):
        finish(*part_items(len(groups_of) - 1, r))
        gathered[r] = dot(one_hot[r], last[r].reshape(q * lanes, width), ((1,), (0,))).astype(BF16)
        grads = dot(feat_t[...], gathered[r], ((1,), (0,))).astype(BF16)
        sum1_a[r] = grads[:, low].reshape(q, strip_rows, half)
        sum1_b[r] = grads[:, high].reshape(q, strip_rows, half)
        start(
            ("y", SUM1 + 2 * r, lambda j: sum1_a.at[r, j], lambda t: sum1_in_a.at[r, t]),
            ("z", SUM1 + 2 * r + 1, lambda j: sum1_b.at[r, j], lambda t: sum1_in_b.at[r, t]),
        )
        sum1_in_a[r, 0] = sum1_a[r, y]
        sum1_in_b[r, 0] = sum1_b[r, z]

    loads[6].wait()
    total = dot(gathered[0], weight[0], ((1,), (1,)))
    for r in range(1, rels):
        total = total + dot(gathered[r], weight[r], ((1,), (1,)))
    share[...] = total.reshape(groups, own_rows, width)
    start(("rel", FEAT, lambda j: share.at[j], lambda t: share_in.at[t]))
    share_in[0] = share[k]

    small = strip_rows // q

    def add_first(r):
        for axis, s, other, me, sums, sums_in, sends, sends_in in (
            ("y", 0, "z", z, sum1_a, sum1_in_a, sum2_a, sum2_in_a),
            ("z", 1, "y", y, sum1_b, sum1_in_b, sum2_b, sum2_in_b),
        ):
            finish((axis, SUM1 + 2 * r + s, lambda j: sums.at[r, j], lambda t, j: sums_in.at[r, t]))
            total = sums_in[r, 0].astype(F32)
            for b in range(1, q):
                total = total + sums_in[r, b].astype(F32)
            sends[r] = total.reshape(q, small, half)
            start((other, SUM2 + 2 * r + s, lambda j: sends.at[r, j], lambda t: sends_in.at[r, t]))
            sends_in[r, 0] = sends[r, me]

    def add_second(r):
        for axis, s, me, sends, sends_in, block in (
            ("z", 0, z, sum2_a, sum2_in_a, block_a), ("y", 1, y, sum2_b, sum2_in_b, block_b),
        ):
            finish((axis, SUM2 + 2 * r + s, lambda j: sends.at[r, j], lambda t, j: sends_in.at[r, t]))
            total = sends_in[r, 0]
            for b in range(1, q):
                total = total + sends_in[r, b]
            total = total * scale
            block[r, me] = jnp.concatenate([total[:, : half // 2], total[:, half // 2 :]], axis=0).astype(BF16)
            start((axis, ALL1 + 2 * r + s, lambda j: block.at[r, me], lambda t: block.at[r, me]))

    stores = []

    def place_of(r, j):
        return pl.ds(pl.multiple_of(r * width + j * strip_rows, strip_rows), strip_rows)

    def gather_last(r):
        for axis, s, me, other, you, block, whole, side in (
            ("z", 0, z, "y", y, block_a, all_a, low), ("y", 1, y, "z", z, block_b, all_b, high),
        ):
            finish((axis, ALL1 + 2 * r + s, lambda j: block.at[r, me], lambda t, j: block.at[r, j]))
            pieces = block[r].astype(F32)
            sides = [pieces[:, i * small : (i + 1) * small, :].reshape(strip_rows, half // 2) for i in (0, 1)]
            whole[r] = jnp.concatenate(sides, axis=1).astype(BF16)
            start((other, ALL2 + 2 * r + s, lambda j: whole.at[r], lambda t: out_rel.at[place_of(r, you), side]))
            stores.append(pltpu.make_async_copy(
                whole.at[r], out_rel.at[place_of(r, you), side], store_sem.at[2 + 2 * r + s]
            ))
            stores[-1].start()

    add_first(0)
    start(("y", SELF1, lambda j: self1.at[j], lambda t: self1_in.at[t]))
    for r in range(1, rels):
        add_first(r)
    add_second(0)
    finish(("y", SELF1, lambda j: self1.at[j], lambda t, j: self1_in.at[t]))
    total = self1_in[0].astype(F32)
    for b in range(1, q):
        total = total + self1_in[b].astype(F32)
    self2[...] = total
    start(("z", SELF2, lambda j: self2, lambda t: self2_in.at[z]))
    self2_in[z] = total
    for r in range(1, rels):
        add_second(r)
    gather_last(0)
    finish(("z", SELF2, lambda j: self2, lambda t, j: self2_in.at[j]))
    total = self2_in[0]
    for b in range(1, q):
        total = total + self2_in[b]
    self3[...] = (total * scale).astype(BF16)
    start(("y", SELF3, lambda j: self3, lambda t: self3_in.at[y]))
    self3_in[y] = self3[...]
    for r in range(1, rels):
        gather_last(r)

    finish(("rel", FEAT, lambda j: share.at[j], lambda t, j: share_in.at[t]))
    total = self_term[...]
    for b in range(groups):
        total = total + share_in[b]
    feat_out[...] = total.astype(BF16)
    stores.append(pltpu.make_async_copy(feat_out, out_feat, store_sem.at[0]))
    stores[-1].start()

    finish(("y", SELF3, lambda j: self3, lambda t, j: self3_in.at[j]))
    for b in range(0, q, 2):
        pair = [self3_in[b + i].astype(F32) for i in (0, 1)]
        wide_rows = [jnp.concatenate([p[:strip], p[strip:]], axis=1) for p in pair]
        self_out[b * strip : (b + 2) * strip, :] = jnp.concatenate(wide_rows, axis=0).astype(BF16)
    stores.append(pltpu.make_async_copy(self_out, out_self, store_sem.at[1]))
    stores[-1].start()

    for r in range(rels):
        finish(
            ("y", ALL2 + 2 * r, lambda j: all_a.at[r], lambda t, j: out_rel.at[place_of(r, j), low]),
            ("z", ALL2 + 2 * r + 1, lambda j: all_b.at[r], lambda t, j: out_rel.at[place_of(r, j), high]),
        )
    for store in stores:
        store.wait()
    for t in range(1, q):
        for axis, me, side, columns, raw in ends:
            pass_on(axis, me, side, t, grad_hbm.at[own, columns], raw).wait_send()
            share_core(side, t, raw).wait_send()


def solution(mesh):
    q = int(round(mesh.shape["nodes"] ** 0.5))
    groups = mesh.shape["rel"]

    def per_device(grad_out, node_feats, rel_weight, self_weight, send_rows, recv_rows, send_counts):
        node_rows, width = grad_out.shape
        rels = rel_weight.shape[0]
        slots = send_rows.shape[3]
        half, lanes = width // 2, q * slots
        strip_rows = width // q
        small = strip_rows // q
        strip = width // groups // q
        own_rows = node_rows // groups
        blocks = q * q
        in_hbm = pl.BlockSpec(memory_space=pltpu.HBM)
        flops = 2 * width * (3 * rels * node_rows * q * lanes + 3 * rels * node_rows * width)

        def two(shape, dtype):
            return [pltpu.VMEM(shape, dtype)] * 2

        outs = pl.pallas_call(
            functools.partial(kernel, q, groups, (node_rows * q * q) ** (-0.5)),
            out_shape=(
                jax.ShapeDtypeStruct((own_rows, width), BF16),
                jax.ShapeDtypeStruct((rels * width, width), BF16),
                jax.ShapeDtypeStruct((width // groups, width), BF16),
            ),
            in_specs=[in_hbm] * 7,
            out_specs=(in_hbm,) * 3,
            scratch_shapes=[
                pltpu.VMEM((node_rows, width), BF16),
                pltpu.VMEM((node_rows, width), BF16),
                pltpu.VMEM((rels, width, width), BF16),
                pltpu.VMEM((width, width), BF16),
                pltpu.VMEM((rels, slots, blocks), jnp.int32),
                pltpu.VMEM((rels, slots, blocks), jnp.int32),
                pltpu.VMEM((rels, 1, blocks), jnp.int32),
            ]
            + two((q, 8, lanes), F32)
            + two((q, 8, lanes), F32)
            + two((q, node_rows, half), BF16)
            + two((q, rels, q, slots, half), BF16)
            + [pltpu.VMEM((rels, q, q, slots, width), BF16)]
            + two((q, 8, lanes), F32)
            + [
                pltpu.VMEM((rels, node_rows, q * lanes), BF16),
                pltpu.VMEM((width, node_rows), BF16),
                pltpu.VMEM((rels, node_rows, width), BF16),
                pltpu.VMEM((width, width), F32),
                pltpu.VMEM((q, 2 * strip, half), BF16),
                pltpu.VMEM((q, 2 * strip, half), BF16),
                pltpu.VMEM((2 * strip, half), F32),
                pltpu.VMEM((q, 2 * strip, half), F32),
                pltpu.VMEM((2 * strip, half), BF16),
                pltpu.VMEM((q, 2 * strip, half), BF16),
                pltpu.VMEM((own_rows, width), F32),
            ]
            + two((groups, own_rows, width), F32)
            + two((rels, q, strip_rows, half), BF16)
            + two((rels, q, strip_rows, half), BF16)
            + two((rels, q, small, half), F32)
            + two((rels, q, small, half), F32)
            + two((rels, q, 2 * small, half // 2), BF16)
            + two((rels, strip_rows, half), BF16)
            + [
                pltpu.VMEM((own_rows, width), BF16),
                pltpu.VMEM((width // groups, width), BF16),
                pltpu.SemaphoreType.DMA((EXCHANGES, max(q, groups))),
                pltpu.SemaphoreType.DMA((EXCHANGES, max(q, groups))),
                pltpu.SemaphoreType.DMA((7,)),
                pltpu.SemaphoreType.DMA((2 + 2 * rels,)),
            ],
            compiler_params=pltpu.CompilerParams(
                collective_id=0, has_side_effects=True, vmem_limit_bytes=60 * 1024 * 1024
            ),
            cost_estimate=pl.CostEstimate(flops=flops, bytes_accessed=4 * 1024 * 1024, transcendentals=0),
        )(
            grad_out, node_feats, rel_weight, self_weight,
            send_rows.transpose(0, 1, 3, 2).reshape(rels, slots, blocks),
            recv_rows.transpose(0, 1, 3, 2).reshape(rels, slots, blocks),
            send_counts,
        )
        return outs[0], outs[1].reshape(rels, width, width), outs[2]

    return jax.shard_map(
        per_device,
        mesh=mesh,
        in_specs=(
            P("nodes", None),
            P("nodes", None),
            P("rel", None, None),
            P(),
            P("rel", "nodes", None, None),
            P("rel", "nodes", None, None),
            P("rel", "nodes", None),
        ),
        out_specs=(P(("nodes", "rel"), None), P("rel", None, None), P("rel", None)),
        check_vma=False,
    )
```

```python
import functools

import jax
import jax.numpy as jnp
from jax import lax
from jax.experimental import pallas as pl
from jax.experimental.pallas import tpu as pltpu
from jax.sharding import PartitionSpec as P

MESH = pl.DeviceIdType.MESH
F32 = jnp.float32
BF16 = jnp.bfloat16

META, RAW, CORE, PART, SUM1, SUM2, ALL1, ALL2, TGT, SELF1, SELF2, SELF3, FEAT = 0, 2, 4, 6, 18, 22, 26, 30, 34, 35, 36, 37, 38
EXCHANGES = 39


def iota(shape, dim):
    return lax.broadcasted_iota(jnp.int32, shape, dim)


def dot(a, b, contract):
    return lax.dot_general(a, b, ((contract[0], contract[1]), ((), ())), preferred_element_type=F32)


def kernel(
    q, groups, scale,
    grad_hbm, feat_hbm, weight_hbm, self_hbm, rows_hbm, targets_hbm, counts_hbm,
    out_feat, out_rel, out_self,
    grad, feat, weight, self_w, rows, targets, counts,
    meta_a, meta_b, meta_in_a, meta_in_b, raw_a, raw_b, part_a, part_b, last,
    tgt_send, tgt_last, one_hot, feat_t, gathered, self_all, self1, self1_in, self2, self2_in, self3, self3_in,
    self_term, share, share_in, sum1_a, sum1_b, sum1_in_a, sum1_in_b, sum2_a, sum2_b, sum2_in_a, sum2_in_b,
    block_a, block_b, all_a, all_b, feat_out, self_out,
    send_sem, recv_sem, load_sem, store_sem,
):
    rels, node_rows, width = gathered.shape
    slots = last.shape[3]
    half, lanes = width // 2, q * slots
    n = lax.axis_index("nodes")
    k = lax.axis_index("rel")
    z, y, core = n // q, n % q, k % 2
    low, high = slice(0, half), slice(half, width)

    def offset(t, count):
        near = (t + 1) // 2
        return (t % 2) * near + (1 - t % 2) * (count - near)

    def along(axis, j):
        return (j * q + y, k) if axis == "z" else ((z * q + j, k) if axis == "y" else (n, j))

    def place(axis):
        return (z, q) if axis == "z" else ((y, q) if axis == "y" else (k, groups))

    def copy(row, t, source, target, device):
        return pltpu.make_async_remote_copy(
            src_ref=source, dst_ref=target, send_sem=send_sem.at[row, t], recv_sem=recv_sem.at[row, t],
            device_id=device, device_id_type=MESH,
        )

    def start(*items, first=1, stop=None):
        def body(t, carry):
            for axis, row, source, target in items:
                me, count = place(axis)
                peer = (me + offset(t, count)) % count
                copy(row, t, source(peer), target(t), along(axis, peer)).start()
            return carry

        lax.fori_loop(first, stop or place(items[0][0])[1], body, 0)

    def finish(*items):
        def body(t, carry):
            for axis, row, source, landing in items:
                me, count = place(axis)
                peer = (me + count - offset(t, count)) % count
                copy(row, t, source(peer), landing(t, peer), along(axis, peer)).wait()
            return carry

        lax.fori_loop(1, place(items[0][0])[1], body, 0)

    barrier = pltpu.get_barrier_semaphore()
    for axis in ("z", "y", "rel"):
        me, count = place(axis)

        def greet(t, carry, axis=axis, me=me, count=count):
            pl.semaphore_signal(barrier, inc=1, device_id=along(axis, (me + t) % count), device_id_type=MESH)
            return carry

        lax.fori_loop(1, count, greet, 0)

    loads = [
        pltpu.make_async_copy(source, target, load_sem.at[i])
        for i, (source, target) in enumerate((
            (rows_hbm, rows), (counts_hbm, counts), (targets_hbm, targets), (grad_hbm, grad),
            (feat_hbm, feat), (self_hbm, self_w), (weight_hbm, weight),
        ))
    ]
    for load in loads:
        load.start()

    pl.semaphore_wait(barrier, 2 * (q - 1) + groups - 1)
    own = pl.ds(pl.multiple_of(core * (node_rows // 2), node_rows // 2), node_rows // 2)
    ends = (("z", z, 0, low, raw_a), ("y", y, 1, high, raw_b))
    ring = range(1, min(3, q))

    def pass_on(axis, me, side, t, source, raw):
        step = 1 if t % 2 else q - 1
        return copy(RAW + side, t, source, raw.at[t, own], along(axis, (me + step) % q))

    def share_core(side, t, raw):
        return copy(CORE + side, t, raw.at[t, own], raw.at[t, own], (n, k + 1 - 2 * core))

    for t in ring:
        for axis, me, side, columns, raw in ends:
            pass_on(axis, me, side, t, grad_hbm.at[own, columns], raw).start()

    node = iota((node_rows, lanes), 0)
    eye = iota((lanes, lanes), 0) == iota((lanes, lanes), 1)
    blocks = q * q
    spread = (iota((slots, lanes), 0) == iota((slots, lanes), 1) % slots).astype(BF16)
    from_z = iota((blocks, lanes), 0) // q == iota((blocks, lanes), 1) // slots
    from_y = iota((blocks, lanes), 0) % q == iota((blocks, lanes), 1) // slots
    meta_a[...] = jnp.zeros_like(meta_a)
    meta_b[...] = jnp.zeros_like(meta_b)
    for load in loads[:3]:
        load.wait()
    for r in range(rels):
        live = iota((slots, blocks), 0) < counts[r]
        picks = dot(jnp.where(live, rows[r], -1).astype(F32).astype(BF16), spread, ((0,), (0,)))
        adds = dot(jnp.where(live, targets[r], -1).astype(F32).astype(BF16), spread, ((0,), (0,)))
        pick_a = jnp.sum(jnp.where(from_y, picks, 0.0).reshape(q, q, lanes), axis=1)
        pick_b = jnp.sum(jnp.where(from_z, picks, 0.0).reshape(q, q, lanes), axis=0)
        add_a = jnp.sum(jnp.where(from_y, adds, 0.0).reshape(q, q, lanes), axis=1)
        hits = jnp.zeros((node_rows, lanes), F32)
        for b in range(q):
            hits = hits + (pick_a[b : b + 1].astype(jnp.int32) == node).astype(F32)
        inverse = 1.0 / jnp.maximum(jnp.sum(hits, axis=1, keepdims=True), 1.0)
        for pick, meta in ((pick_a, meta_a), (pick_b, meta_b)):
            for b in range(q):
                row = pick[b : b + 1]
                meta[b, r : r + 1, :] = row
                meta[b, rels + r : rels + r + 1, :] = jnp.sum(
                    jnp.where(row.astype(jnp.int32) == node, inverse, 0.0), axis=0, keepdims=True
                )
        for b in range(q):
            meta_a[b, 2 * rels + r : 2 * rels + r + 1, :] = add_a[b : b + 1]

    start(
        ("z", META, lambda j: meta_a.at[j], lambda t: meta_in_a.at[t]),
        ("y", META + 1, lambda j: meta_b.at[j], lambda t: meta_in_b.at[t]),
    )
    loads[3].wait()
    meta_in_a[0] = meta_a[z]
    meta_in_b[0] = meta_b[y]
    raw_a[0] = grad[:, low]
    raw_b[0] = grad[:, high]

    def forward(t):
        for axis, me, side, columns, raw in ends:
            pass_on(axis, me, side, t, grad_hbm.at[own, columns], raw).wait_recv()
            if t + 2 < q:
                pass_on(axis, me, side, t + 2, raw.at[t, own], raw).start()
            share_core(side, t, raw).start()

    def pick(t):
        other = pl.ds(pl.multiple_of((1 - core) * (node_rows // 2), node_rows // 2), node_rows // 2)
        for side, raw, meta, part in ((0, raw_a, meta_in_a, part_a), (1, raw_b, meta_in_b, part_b)):
            if t > 0:
                copy(CORE + side, t, raw.at[t, own], raw.at[t, other], (n, k)).wait_recv()
            for r in range(rels):
                hot = (meta[t, r : r + 1, :].astype(jnp.int32) == node).astype(BF16)
                factor = jnp.sum(jnp.where(eye, meta[t, rels + r : rels + r + 1, :], 0.0), axis=1, keepdims=True)
                message = (dot(hot, raw[t], ((0,), (0,))) * factor).astype(BF16)
                part[:, r, t] = message.reshape(q, slots, half)

    groups_of = [(0, 1)] + [(t, min(t + 2, q)) for t in range(1, q, 2)]

    def part_items(g, r=None):
        span = pl.ds(groups_of[g][0], groups_of[g][1] - groups_of[g][0])
        which = slice(None) if r is None else r
        row = PART + 2 * g + 2 * (r or 0)
        return (
            ("y", row, lambda j: part_a.at[j, which, span], lambda t, j=0: last.at[which, t, span, :, low]),
            ("z", row + 1, lambda j: part_b.at[j, which, span], lambda t, j=0: last.at[which, span, t, :, high]),
        )

    pick(0)
    start(*part_items(0))

    for t in ring:
        forward(t)
    finish(
        ("z", META, lambda j: meta_a.at[j], lambda t, j: meta_in_a.at[t]),
        ("y", META + 1, lambda j: meta_b.at[j], lambda t, j: meta_in_b.at[t]),
    )
    wide = q * lanes
    same_slot = iota((lanes, wide), 0) == (iota((lanes, wide), 1) // lanes) * slots + iota((lanes, wide), 1) % slots
    same_from = iota((q, wide), 0) == (iota((q, wide), 1) // slots) % q
    tgt_send[...] = jnp.zeros_like(tgt_send)
    for r in range(rels):
        copies = dot(meta_in_a[:, 2 * rels + r, :].astype(BF16), same_slot.astype(BF16), ((1,), (0,)))
        row = jnp.sum(jnp.where(same_from, copies, 0.0), axis=0, keepdims=True)
        for b in range(q):
            tgt_send[b, r : r + 1, :] = row[:, b * lanes : (b + 1) * lanes]
    start(("y", TGT, lambda j: tgt_send.at[j], lambda t: tgt_last.at[t]))
    tgt_last[0] = tgt_send[y]

    for g in range(1, len(groups_of)):
        for t in range(*groups_of[g]):
            if t not in ring:
                forward(t)
        for t in range(*groups_of[g]):
            pick(t)
        if g < len(groups_of) - 1:
            start(*part_items(g))
    for r in range(rels):
        start(*part_items(len(groups_of) - 1, r))
    for r in range(rels):
        last[r, 0, :, :, low] = part_a[y, r]
        last[r, :, 0, :, high] = part_b[z, r]

    loads[4].wait()
    feat_t[...] = feat[...].T
    self_all[...] = dot(feat_t[...], grad[...], ((1,), (0,)))
    self_rows = width // groups
    strip = self_rows // q
    for b in range(q):
        mine = self_all[pl.ds(pl.multiple_of(k * self_rows + b * strip, strip), strip), :]
        self1[b] = jnp.concatenate([mine[:, low], mine[:, high]], axis=0).astype(BF16)
    start(("y", SELF1, lambda j: self1.at[j], lambda t: self1_in.at[t]))
    self1_in[0] = self1[y]
    loads[5].wait()
    own_rows = node_rows // groups
    mine = pl.ds(pl.multiple_of(k * own_rows, own_rows), own_rows)
    self_term[...] = dot(grad[mine, :], self_w[...], ((1,), (1,)))

    finish(("y", TGT, lambda j: tgt_send.at[j], lambda t, j: tgt_last.at[t]))
    for r in range(rels):
        for b in range(q):
            one_hot[r, :, b * lanes : (b + 1) * lanes] = (
                tgt_last[b, r : r + 1, :].astype(jnp.int32) == node
            ).astype(BF16)

    for g in range(len(groups_of) - 1):
        finish(*part_items(g))
    strip_rows = width // q
    for r in range(rels):
        finish(*part_items(len(groups_of) - 1, r))
        gathered[r] = dot(one_hot[r], last[r].reshape(q * lanes, width), ((1,), (0,))).astype(BF16)
        grads = dot(feat_t[...], gathered[r], ((1,), (0,))).astype(BF16)
        sum1_a[r] = grads[:, low].reshape(q, strip_rows, half)
        sum1_b[r] = grads[:, high].reshape(q, strip_rows, half)
        start(
            ("y", SUM1 + 2 * r, lambda j: sum1_a.at[r, j], lambda t: sum1_in_a.at[r, t]),
            ("z", SUM1 + 2 * r + 1, lambda j: sum1_b.at[r, j], lambda t: sum1_in_b.at[r, t]),
        )
        sum1_in_a[r, 0] = sum1_a[r, y]
        sum1_in_b[r, 0] = sum1_b[r, z]

    loads[6].wait()
    total = dot(gathered[0], weight[0], ((1,), (1,)))
    for r in range(1, rels):
        total = total + dot(gathered[r], weight[r], ((1,), (1,)))
    share[...] = total.reshape(groups, own_rows, width)
    start(("rel", FEAT, lambda j: share.at[j], lambda t: share_in.at[t]))
    share_in[0] = share[k]

    finish(("y", SELF1, lambda j: self1.at[j], lambda t, j: self1_in.at[t]))
    total = self1_in[0].astype(F32)
    for b in range(1, q):
        total = total + self1_in[b].astype(F32)
    self2[...] = total
    start(("z", SELF2, lambda j: self2, lambda t: self2_in.at[z]))
    self2_in[z] = total

    small = strip_rows // q

    def add_first(r):
        for axis, s, other, me, sums, sums_in, sends, sends_in in (
            ("y", 0, "z", z, sum1_a, sum1_in_a, sum2_a, sum2_in_a),
            ("z", 1, "y", y, sum1_b, sum1_in_b, sum2_b, sum2_in_b),
        ):
            finish((axis, SUM1 + 2 * r + s, lambda j: sums.at[r, j], lambda t, j: sums_in.at[r, t]))
            total = sums_in[r, 0].astype(F32)
            for b in range(1, q):
                total = total + sums_in[r, b].astype(F32)
            sends[r] = total.reshape(q, small, half)
            start((other, SUM2 + 2 * r + s, lambda j: sends.at[r, j], lambda t: sends_in.at[r, t]))
            sends_in[r, 0] = sends[r, me]

    def add_second(r):
        for axis, s, me, sends, sends_in, block in (
            ("z", 0, z, sum2_a, sum2_in_a, block_a), ("y", 1, y, sum2_b, sum2_in_b, block_b),
        ):
            finish((axis, SUM2 + 2 * r + s, lambda j: sends.at[r, j], lambda t, j: sends_in.at[r, t]))
            total = sends_in[r, 0]
            for b in range(1, q):
                total = total + sends_in[r, b]
            total = total * scale
            block[r, me] = jnp.concatenate([total[:, : half // 2], total[:, half // 2 :]], axis=0).astype(BF16)
            start((axis, ALL1 + 2 * r + s, lambda j: block.at[r, me], lambda t: block.at[r, me]))

    stores = []

    def place_of(r, j):
        return pl.ds(pl.multiple_of(r * width + j * strip_rows, strip_rows), strip_rows)

    def gather_last(r):
        for axis, s, me, other, you, block, whole, side in (
            ("z", 0, z, "y", y, block_a, all_a, low), ("y", 1, y, "z", z, block_b, all_b, high),
        ):
            finish((axis, ALL1 + 2 * r + s, lambda j: block.at[r, me], lambda t, j: block.at[r, j]))
            pieces = block[r].astype(F32)
            sides = [pieces[:, i * small : (i + 1) * small, :].reshape(strip_rows, half // 2) for i in (0, 1)]
            whole[r] = jnp.concatenate(sides, axis=1).astype(BF16)
            start((other, ALL2 + 2 * r + s, lambda j: whole.at[r], lambda t: out_rel.at[place_of(r, you), side]))
            stores.append(pltpu.make_async_copy(
                whole.at[r], out_rel.at[place_of(r, you), side], store_sem.at[2 + 2 * r + s]
            ))
            stores[-1].start()

    add_first(0)
    for r in range(1, rels):
        add_first(r)
    finish(("z", SELF2, lambda j: self2, lambda t, j: self2_in.at[j]))
    total = self2_in[0]
    for b in range(1, q):
        total = total + self2_in[b]
    self3[...] = (total * scale).astype(BF16)
    start(("y", SELF3, lambda j: self3, lambda t: self3_in.at[y]))
    self3_in[y] = self3[...]
    add_second(0)
    for r in range(1, rels):
        add_second(r)
    gather_last(0)
    for r in range(1, rels):
        gather_last(r)

    finish(("rel", FEAT, lambda j: share.at[j], lambda t, j: share_in.at[t]))
    total = self_term[...]
    for b in range(groups):
        total = total + share_in[b]
    feat_out[...] = total.astype(BF16)
    stores.append(pltpu.make_async_copy(feat_out, out_feat, store_sem.at[0]))
    stores[-1].start()

    finish(("y", SELF3, lambda j: self3, lambda t, j: self3_in.at[j]))
    for b in range(0, q, 2):
        pair = [self3_in[b + i].astype(F32) for i in (0, 1)]
        wide_rows = [jnp.concatenate([p[:strip], p[strip:]], axis=1) for p in pair]
        self_out[b * strip : (b + 2) * strip, :] = jnp.concatenate(wide_rows, axis=0).astype(BF16)
    stores.append(pltpu.make_async_copy(self_out, out_self, store_sem.at[1]))
    stores[-1].start()

    for r in range(rels):
        finish(
            ("y", ALL2 + 2 * r, lambda j: all_a.at[r], lambda t, j: out_rel.at[place_of(r, j), low]),
            ("z", ALL2 + 2 * r + 1, lambda j: all_b.at[r], lambda t, j: out_rel.at[place_of(r, j), high]),
        )
    for store in stores:
        store.wait()
    for t in range(1, q):
        for axis, me, side, columns, raw in ends:
            pass_on(axis, me, side, t, grad_hbm.at[own, columns], raw).wait_send()
            share_core(side, t, raw).wait_send()


def solution(mesh):
    q = int(round(mesh.shape["nodes"] ** 0.5))
    groups = mesh.shape["rel"]

    def per_device(grad_out, node_feats, rel_weight, self_weight, send_rows, recv_rows, send_counts):
        node_rows, width = grad_out.shape
        rels = rel_weight.shape[0]
        slots = send_rows.shape[3]
        half, lanes = width // 2, q * slots
        strip_rows = width // q
        small = strip_rows // q
        strip = width // groups // q
        own_rows = node_rows // groups
        blocks = q * q
        in_hbm = pl.BlockSpec(memory_space=pltpu.HBM)
        flops = 2 * width * (3 * rels * node_rows * q * lanes + 3 * rels * node_rows * width)

        def two(shape, dtype):
            return [pltpu.VMEM(shape, dtype)] * 2

        outs = pl.pallas_call(
            functools.partial(kernel, q, groups, (node_rows * q * q) ** (-0.5)),
            out_shape=(
                jax.ShapeDtypeStruct((own_rows, width), BF16),
                jax.ShapeDtypeStruct((rels * width, width), BF16),
                jax.ShapeDtypeStruct((width // groups, width), BF16),
            ),
            in_specs=[in_hbm] * 7,
            out_specs=(in_hbm,) * 3,
            scratch_shapes=[
                pltpu.VMEM((node_rows, width), BF16),
                pltpu.VMEM((node_rows, width), BF16),
                pltpu.VMEM((rels, width, width), BF16),
                pltpu.VMEM((width, width), BF16),
                pltpu.VMEM((rels, slots, blocks), jnp.int32),
                pltpu.VMEM((rels, slots, blocks), jnp.int32),
                pltpu.VMEM((rels, 1, blocks), jnp.int32),
            ]
            + two((q, 8, lanes), F32)
            + two((q, 8, lanes), F32)
            + two((q, node_rows, half), BF16)
            + two((q, rels, q, slots, half), BF16)
            + [pltpu.VMEM((rels, q, q, slots, width), BF16)]
            + two((q, 8, lanes), F32)
            + [
                pltpu.VMEM((rels, node_rows, q * lanes), BF16),
                pltpu.VMEM((width, node_rows), BF16),
                pltpu.VMEM((rels, node_rows, width), BF16),
                pltpu.VMEM((width, width), F32),
                pltpu.VMEM((q, 2 * strip, half), BF16),
                pltpu.VMEM((q, 2 * strip, half), BF16),
                pltpu.VMEM((2 * strip, half), F32),
                pltpu.VMEM((q, 2 * strip, half), F32),
                pltpu.VMEM((2 * strip, half), BF16),
                pltpu.VMEM((q, 2 * strip, half), BF16),
                pltpu.VMEM((own_rows, width), F32),
            ]
            + two((groups, own_rows, width), F32)
            + two((rels, q, strip_rows, half), BF16)
            + two((rels, q, strip_rows, half), BF16)
            + two((rels, q, small, half), F32)
            + two((rels, q, small, half), F32)
            + two((rels, q, 2 * small, half // 2), BF16)
            + two((rels, strip_rows, half), BF16)
            + [
                pltpu.VMEM((own_rows, width), BF16),
                pltpu.VMEM((width // groups, width), BF16),
                pltpu.SemaphoreType.DMA((EXCHANGES, max(q, groups))),
                pltpu.SemaphoreType.DMA((EXCHANGES, max(q, groups))),
                pltpu.SemaphoreType.DMA((7,)),
                pltpu.SemaphoreType.DMA((2 + 2 * rels,)),
            ],
            compiler_params=pltpu.CompilerParams(
                collective_id=0, has_side_effects=True, vmem_limit_bytes=60 * 1024 * 1024
            ),
            cost_estimate=pl.CostEstimate(flops=flops, bytes_accessed=4 * 1024 * 1024, transcendentals=0),
        )(
            grad_out, node_feats, rel_weight, self_weight,
            send_rows.transpose(0, 1, 3, 2).reshape(rels, slots, blocks),
            recv_rows.transpose(0, 1, 3, 2).reshape(rels, slots, blocks),
            send_counts,
        )
        return outs[0], outs[1].reshape(rels, width, width), outs[2]

    return jax.shard_map(
        per_device,
        mesh=mesh,
        in_specs=(
            P("nodes", None),
            P("nodes", None),
            P("rel", None, None),
            P(),
            P("rel", "nodes", None, None),
            P("rel", "nodes", None, None),
            P("rel", "nodes", None),
        ),
        out_specs=(P(("nodes", "rel"), None), P("rel", None, None), P("rel", None)),
        check_vma=False,
    )
```
